32 devices in a mesh: group: 4 (over x, core), orb: 8 (over z, y).
Axes of the slice: x: 2, y: 2, z: 4, core: 2. Of those that a mesh axis runs over, the one named last changes fastest.
Arguments:
- orbitals: bfloat16 [96, 64, 1024], P(None, 'orb'), may hold values from -40 to 40
- potential: float32 [64, 1024], P('orb'), may hold values from -5 to 5
- box_shift: int32 [96], replicated, may hold values from 0 to 31, as said below
- pair_partner: int32 [24, 56], replicated, may hold values from -1 to 191, as said below
- pair_member: int32 [24, 56], replicated, may hold values from 0 to 7
Outputs:
- hamiltonian: float32 [96, 64, 1024], P(None, 'orb')
The draws below stay inside these ranges and needn't reach their ends.
Inputs may be any that keep to these rules, and one draw needn't show every extreme that they name: Exactly 24 colors have each value of box_shift // 8. `pair_partner`: -1 marks an empty slot; a live slot p of block b names a home orbital of slab (b // 3 + p // 8 - 3) mod (8); some block has every slot live.
All inputs are finite; a program needn't handle non-finite values.
Results may differ from the reference program's by a relative error of at most 0.0004.
Values may be sent and summed in bfloat16 or wider, within the bound.
No kernel may reach another device: no remote copies, remote signals or barrier semaphores. Data moves between devices by JAX's collectives and lax.ppermute only.
A program may use at most 128 MiB of HBM per device.

```python
import jax
import jax.numpy as jnp
from jax import lax

B = 32
CX = 8
MEMBERS = 8
QCAP = 8
W = 4
EXCH = 3
HOME = 24
NCOL = 96
NX = 64
PER = 2
NBLK = 24
PCAP = 56


def color_layout(key):
    shuffled = jax.random.permutation(jax.random.fold_in(key, 7), NCOL)
    classes = (shuffled % W).astype(jnp.int32)
    subrows = jax.random.randint(jax.random.fold_in(key, 8), (NCOL,), 0, CX, dtype=jnp.int32)
    return (classes, classes * CX + subrows)


def draw_box_shift(key, part):
    classes, shifts = color_layout(key)
    return shifts.astype(jnp.int32)


def draw_pair_partner(key, part):
    classes, shifts = color_layout(key)
    colors = jnp.arange(NCOL, dtype=jnp.int32)
    color_order = jnp.argsort(classes * NCOL + colors).astype(jnp.int32).reshape(W, HOME)
    slab_total = NX // CX
    block_slab = jnp.arange(NBLK, dtype=jnp.int32) // EXCH
    slot_reach = jnp.arange(PCAP, dtype=jnp.int32) // QCAP - (W - 1)
    partner_slab = (block_slab[:, None] + slot_reach[None, :]) % slab_total
    home_pick = jax.random.randint(jax.random.fold_in(key, 9), (NBLK, PCAP), 0, HOME, dtype=jnp.int32)
    partner_color = color_order[partner_slab % W, home_pick]
    partner_id = partner_color * PER + partner_slab // W
    levels = jax.random.randint(jax.random.fold_in(key, 10), (NBLK,), 0, 101, dtype=jnp.int32)
    cutoff = levels * levels * levels
    full_block = jax.random.randint(jax.random.fold_in(key, 11), (), 0, NBLK, dtype=jnp.int32)
    cutoff = jnp.where(jnp.arange(NBLK, dtype=jnp.int32) == full_block, 1000001, cutoff)
    coin_draws = jax.random.randint(jax.random.fold_in(key, 12), (NBLK, PCAP), 0, 1000000, dtype=jnp.int32)
    return jnp.where(coin_draws < cutoff[:, None], partner_id, -1).astype(jnp.int32)


def smooth_axis(values, axis_no, wrapped):
    reach_cells = 3
    kernel_taps = jnp.exp(-0.5 * jnp.arange(-reach_cells, reach_cells + 1, dtype=jnp.float32) ** 2)
    kernel_taps = kernel_taps / jnp.sqrt(jnp.sum(kernel_taps * kernel_taps))
    length = values.shape[axis_no]
    widths = [(0, 0)] * values.ndim
    widths[axis_no] = (reach_cells, reach_cells)
    padded = jnp.pad(values, widths)
    smoothed = jnp.zeros_like(values)
    for index_no in range(2 * reach_cells + 1):
        offset = index_no - reach_cells
        if wrapped:
            shifted = jnp.roll(values, offset, axis=axis_no)
        else:
            shifted = lax.slice_in_dim(padded, reach_cells - offset, reach_cells - offset + length, axis=axis_no)
        smoothed = smoothed + kernel_taps[index_no] * shifted
    return smoothed


def draw_orbitals(key, part):
    noise_key = jax.random.fold_in(key, 21)
    noise = jax.random.truncated_normal(noise_key, -4.0, 4.0, (NCOL, NX, B, B), jnp.float32)
    color_scale = jnp.ones((NCOL,), jnp.float32)
    smoothed = smooth_axis(noise, 1, True)
    smoothed = smooth_axis(smoothed, 2, False)
    smoothed = smooth_axis(smoothed, 3, False)
    fields = 1.5 * color_scale[:, None, None, None] * smoothed
    return fields.reshape(NCOL, NX, B * B).astype(jnp.bfloat16)


def with_ends(values, key, low, high):
    spot = [jax.random.randint(jax.random.fold_in(key, axis), (), 0, length) for axis, length in enumerate(values.shape)]
    widest = values.shape.index(max(values.shape))
    beside = spot[:widest] + [(spot[widest] + 1) % values.shape[widest]] + spot[widest + 1:]
    return values.at[tuple(spot)].set(low).at[tuple(beside)].set(high)


def block_levels(key, dims, shards, low, high):
    gain, own = 1.0, jax.random.fold_in(key, 6)
    for dim, parts in shards:
        heights = jnp.exp(jax.random.uniform(jax.random.fold_in(own, dim), (parts,), jnp.float32, low / len(shards), high / len(shards)))
        gain = gain * jnp.repeat(heights, dims[dim] // parts).reshape([-1 if axis == dim else 1 for axis in range(len(dims))])
    return gain


def scatter_about(key, dims, spread, most, split=(), kind=jnp.bfloat16):
    result = spread * jax.random.normal(key, dims, jnp.float32)
    if split:
        result = result * block_levels(key, dims, split, -0.22, 0.18)
    return jnp.clip(result, -most, most).astype(kind)


def setup_inputs(seed: int = 0) -> dict:
    arg_keys = jax.random.split(jax.random.key(seed), 6)
    return {
        "orbitals": draw_orbitals(jax.random.fold_in(arg_keys[5], 71), 0),
        "potential": scatter_about(arg_keys[1], (NX, B * B), 1.0, 5.0, ((0, 8),), jnp.float32),
        "box_shift": draw_box_shift(jax.random.fold_in(arg_keys[5], 71), 0),
        "pair_partner": draw_pair_partner(jax.random.fold_in(arg_keys[5], 71), 0),
        "pair_member": with_ends(jax.random.randint(arg_keys[4], (NBLK, PCAP), 0, MEMBERS), jax.random.fold_in(arg_keys[4], 1), 0, MEMBERS - 1).astype(jnp.int32),
    }


lap_weights = (-5369.0 / 1800.0, 12.0 / 7.0, -15.0 / 56.0, 10.0 / 189.0, -1.0 / 112.0, 2.0 / 1925.0, -1.0 / 16632.0)
stencil_reach = 6
mixing = 0.25

def sine_rows(box_edge):
    counter = jnp.arange(1, box_edge + 1, dtype=jnp.float32)
    angles = jnp.pi * counter[:, None] * counter[None, :] / (box_edge + 1)
    return jnp.sqrt(2.0 / (box_edge + 1)) * jnp.sin(angles)

def mode_sums(box_edge):
    counter = jnp.arange(1, box_edge + 1, dtype=jnp.float32)
    single = 2.0 - 2.0 * jnp.cos(jnp.pi * counter / (box_edge + 1))
    cube_sum = single[:, None, None] + single[None, :, None] + single[None, None, :]
    return cube_sum.reshape(box_edge, box_edge * box_edge)

def sine_cube(values, sine_mat):
    box_edge = sine_mat.shape[0]
    for rotation in range(3):
        values = jnp.dot(sine_mat, values, precision=lax.Precision.HIGHEST)
        values = values.reshape(box_edge, box_edge, box_edge).transpose(1, 2, 0).reshape(box_edge, box_edge * box_edge)
    return values

def pair_term(member_box, partner_box, offset, sine_mat, mode_sum):
    box_edge = sine_mat.shape[0]
    padded = jnp.pad(partner_box, ((box_edge, box_edge), (0, 0)))
    shifted = lax.dynamic_slice_in_dim(padded, (box_edge - offset).astype(jnp.int32), box_edge, 0).astype(jnp.float32)
    density = member_box.astype(jnp.float32) * shifted
    solved = sine_cube(sine_cube(density, sine_mat) / mode_sum, sine_mat)
    return -mixing * solved * shifted

def cut_along(padded, axis_no, signed, box_edge):
    starts = [0, stencil_reach, stencil_reach, stencil_reach]
    starts[axis_no] = stencil_reach + signed
    limits = [padded.shape[0]] + [starts[index_no] + box_edge for index_no in (1, 2, 3)]
    return lax.slice(padded, starts, limits)

def second_difference(boxes):
    box_edge = boxes.shape[1]
    padded = jnp.pad(boxes, ((0, 0), (stencil_reach, stencil_reach), (stencil_reach, stencil_reach), (stencil_reach, stencil_reach)))
    summed = 3.0 * lap_weights[0] * boxes
    for offset in range(1, stencil_reach + 1):
        for axis_no in (1, 2, 3):
            summed = summed + lap_weights[offset] * (cut_along(padded, axis_no, offset, box_edge) + cut_along(padded, axis_no, -offset, box_edge))
    return summed

def align_rows(values, row_start):
    doubled = jnp.concatenate([values, values], axis=0)
    return lax.dynamic_slice_in_dim(doubled, row_start.astype(jnp.int32), NX, 0)

def reference(orbitals, potential, box_shift, pair_partner, pair_member):
    starts = box_shift.astype(jnp.int32)

    def local_color(packed):
        orbit_rows, row_start = packed
        aligned = align_rows(orbit_rows, row_start).astype(jnp.float32).reshape(PER, B, B, B)
        field_pot = align_rows(potential, row_start).reshape(PER, B, B, B)
        kinetic = -0.5 * second_difference(aligned)
        return (kinetic + field_pot * aligned).reshape(NX, B * B)
    local_parts = lax.map(local_color, (orbitals, starts))

    def align_color(packed):
        return align_rows(packed[0], packed[1])
    aligned_orbs = lax.map(align_color, (orbitals, starts)).reshape(NCOL, PER, B, B * B)
    classes = box_shift // CX
    color_order = jnp.argsort(classes * NCOL + jnp.arange(NCOL, dtype=jnp.int32)).astype(jnp.int32).reshape(W, HOME)
    flat_partner = pair_partner.reshape(-1)
    flat_member = pair_member.reshape(-1)
    slot_count = NBLK * PCAP
    living = flat_partner >= 0
    slot_order = jnp.argsort(jnp.where(living, 0, 1) * slot_count + jnp.arange(slot_count, dtype=jnp.int32)).astype(jnp.int32)
    live_count = jnp.sum(living.astype(jnp.int32))
    sine_mat = sine_rows(B)
    mode_sum = mode_sums(B)

    def add_pair(counter, accum):
        slot_id = slot_order[counter]
        block_id = slot_id // PCAP
        slab_id = block_id // EXCH
        member_at = block_id % EXCH * MEMBERS + flat_member[slot_id]
        member_color = color_order[slab_id % W, member_at]
        member_index = slab_id // W
        partner = flat_partner[slot_id]
        partner_color = partner // PER
        partner_index = partner % PER
        member_anchor = member_index * B + box_shift[member_color]
        partner_anchor = partner_index * B + box_shift[partner_color]
        offset = (partner_anchor - member_anchor + NX // 2) % NX - NX // 2
        pair_value = pair_term(aligned_orbs[member_color, member_index], aligned_orbs[partner_color, partner_index], offset, sine_mat, mode_sum)
        current = accum[member_color, member_index]
        return accum.at[member_color, member_index].set(current + pair_value)
    exchange = lax.fori_loop(0, live_count, add_pair, jnp.zeros((NCOL, PER, B, B * B), jnp.float32))
    combined = local_parts + exchange.reshape(NCOL, NX, B * B)

    def unalign(packed):
        return align_rows(packed[0], (NX - packed[1]) % NX)
    return lax.map(unalign, (combined, starts))
```

```python
import functools
import math

import jax
import jax.numpy as jnp
import numpy as np
from jax import lax
from jax.experimental import pallas as pl
from jax.experimental.pallas import tpu as pltpu
from jax.sharding import PartitionSpec as P

lap_weights = (
    -5369.0 / 1800.0,
    12.0 / 7.0,
    -15.0 / 56.0,
    10.0 / 189.0,
    -1.0 / 112.0,
    2.0 / 1925.0,
    -1.0 / 16632.0,
)
stencil_reach = 6
mixing = 0.25
f32, bf16, i32 = jnp.float32, jnp.bfloat16, jnp.int32
kin_colors = 8
EMPTY = -(1 << 20)


def split_np(values):
    head = np.asarray(values, np.float32).astype(bf16)
    rest = (values - head.astype(np.float64)).astype(np.float32).astype(bf16)
    return np.stack([head, rest])


def split2(x):
    head = x.astype(bf16)
    return head, (x - head.astype(f32)).astype(bf16)


def dot(a, b):
    return jnp.dot(a, b, preferred_element_type=f32)


def dot3(a, b):
    return dot(a[0], b[0]) + (dot(a[0], b[1]) + dot(a[1], b[0]))


class Sizes:
    def __init__(self, orbitals, pair_partner, groups, slabs):
        self.colors, self.rows, self.cells = orbitals.shape
        self.groups, self.slabs = groups, slabs
        self.box = math.isqrt(self.cells)
        self.width = self.box // self.rows
        self.span = self.width + 1
        self.mid = self.width // 2
        self.home = self.colors // self.width
        self.blocks = pair_partner.shape[0] // slabs
        self.members = self.home // self.blocks
        self.slots = pair_partner.shape[1]
        self.grid = slabs * self.rows
        self.per = self.grid // self.box
        self.part = self.colors // groups
        self.own = self.home // groups
        self.frame = self.span * self.rows
        self.batch = max(1, 256 // self.frame)
        self.cap = -(-self.blocks * self.slots // self.batch) * self.batch + self.batch


def butterfly_order(groups):
    order, step = [0], groups // 2
    while step:
        order += [o ^ step for o in order]
        step //= 2
    return order


def sine_matrix(box):
    count = np.arange(1, box + 1)
    return np.sqrt(2.0 / (box + 1)) * np.sin(np.pi * np.outer(count, count) / (box + 1))


def pair_tables(z):
    box, half = z.box, z.box // 2
    sine = sine_matrix(box)
    side = [np.arange(half), box - 1 - np.arange(half)]
    order = np.concatenate([(y[:, None] * box + x[None, :]).reshape(-1) for y in side for x in side])
    regroup = np.zeros((z.cells, z.cells))
    regroup[order, np.arange(z.cells)] = 1.0
    halves = [sine[0::2, :half], sine[1::2, :half]]
    forward = np.stack([np.kron(a, b).T for a in halves for b in halves])
    backward = np.stack([m.T for m in forward])
    single = 2.0 - 2.0 * np.cos(np.pi * np.arange(1, box + 1) / (box + 1))
    modes = [(single[py::2][:, None] + single[pz::2][None, :]).reshape(-1) for py in (0, 1) for pz in (0, 1)]
    scale = -mixing / (single[:, None] + np.concatenate(modes)[None, :])
    into = np.zeros((z.rows, box, z.batch * z.frame))
    back = np.zeros((z.rows, z.frame, z.batch * box))
    for sub in range(z.rows):
        for i in range(z.batch):
            into[sub, :, i * z.frame + sub : i * z.frame + sub + box] = sine
            back[sub, sub : sub + box, i * box : (i + 1) * box] = sine.T
    return dict(
        regroup=regroup.astype(bf16),
        ungroup=regroup.T.astype(bf16),
        forward=split_np(forward),
        backward=split_np(backward),
        scale=scale.astype(np.float32),
        into=into.astype(np.float32),
        back=back.astype(np.float32),
    )


def stencil_tables(z):
    box, rows = z.box, z.rows
    band = np.zeros((box, box))
    for off in range(1, stencil_reach + 1):
        band += lap_weights[off] * (np.eye(box, k=off) + np.eye(box, k=-off))
    eye = np.eye(box)
    plane = -0.5 * (3.0 * lap_weights[0] * np.eye(z.cells) + np.kron(band, eye) + np.kron(eye, band))
    along = np.zeros((box, rows, 3 * kin_colors * rows))
    for start in range(box):
        for x in range(rows):
            for y in range(-rows, 2 * rows):
                off = abs(y - x)
                if off and off <= stencil_reach and (x - start) // box == (y - start) // box:
                    for i in range(kin_colors):
                        at = ((y + rows) // rows) * kin_colors * rows + i * rows + y % rows
                        along[start, x, at] = -0.5 * lap_weights[off]
    return split_np(plane), along.astype(np.float32)


def plan_kernel(z, ids, shift, partner, member, count_ref, slot_ref, mine_ref, src_ref, order, filled):
    q, g = ids[0], ids[1]
    o = lax.rem(q + z.slabs - z.mid, z.slabs)
    for c in range(z.width):
        filled[c] = 0

    def color_step(c, _):
        cls = shift[c] // z.rows
        n = filled[cls]
        filled[cls] = n + 1
        order[cls, n] = c
        back = lax.rem(q - cls + z.slabs * z.width, z.width)
        src_ref[c] = lax.rem(n, z.groups) * z.width * z.own + back * z.own + n // z.groups
        return 0

    lax.fori_loop(0, z.colors, color_step, 0)
    home_class = lax.rem(o, z.width)
    for m in range(z.own):
        c = order[home_class, m * z.groups + g]
        mine_ref[0, m] = c
        mine_ref[1, m] = lax.rem(shift[c], z.rows)
    total = jnp.int32(0)
    for t in range(z.blocks):

        def slot_step(p, total, t=t):
            j = partner[o * z.blocks + t, p]
            n = t * z.members + member[o * z.blocks + t, p]
            live = jnp.logical_and(j >= 0, lax.rem(n, z.groups) == g)
            j = jnp.maximum(j, 0)
            cj = j // z.per
            sub = lax.rem(shift[order[home_class, n]], z.rows)
            there = (j - cj * z.per) * z.box + shift[cj]
            d = there - (o * z.rows + sub) + z.grid // 2
            d = lax.rem(d + z.grid, z.grid) - z.grid // 2
            slot_ref[0, total] = n // z.groups
            slot_ref[1, total] = cj
            slot_ref[2, total] = sub + d
            slot_ref[3, total] = sub
            return total + live.astype(i32)

        total = lax.fori_loop(0, z.slots, slot_step, total)
    count_ref[0] = total
    for i in range(z.batch):
        slot_ref[0, total + i] = 0
        slot_ref[1, total + i] = 0
        slot_ref[2, total + i] = EMPTY
        slot_ref[3, total + i] = 0


def plan(z, ids, shift, partner, member):
    smem = pl.BlockSpec(memory_space=pltpu.SMEM)
    return pl.pallas_call(
        functools.partial(plan_kernel, z),
        out_shape=(
            jax.ShapeDtypeStruct((1,), i32),
            jax.ShapeDtypeStruct((4, z.cap), i32),
            jax.ShapeDtypeStruct((2, z.own), i32),
            jax.ShapeDtypeStruct((z.colors,), i32),
        ),
        in_specs=[smem] * 4,
        out_specs=(smem,) * 4,
        scratch_shapes=[pltpu.SMEM((z.width, z.colors), i32), pltpu.SMEM((z.width,), i32)],
        name="plan",
    )(ids, shift, partner, member)


def pair_kernel(z, ids, count, slots, mine, here, *rest):
    pieces, rest = rest[: (z.span - 1) * z.groups], rest[(z.span - 1) * z.groups :]
    (regroup, ungroup, forward, backward, scale, into, back), rest = rest[:7], rest[7:]
    outs, rest = rest[: z.span], rest[z.span :]
    window, raw, own, held, acc, sems = rest
    g = ids[1]
    order = butterfly_order(z.groups)
    copies = [pltpu.make_async_copy(here, window.at[z.mid], sems.at[0])]
    for k in range(z.span - 1):
        slab = k if k < z.mid else k + 1
        for p in range(z.groups):
            at = (g ^ order[p]) * z.part
            copies.append(
                pltpu.make_async_copy(
                    pieces[k * z.groups + p], window.at[slab, pl.ds(at, z.part)], sems.at[len(copies)]
                )
            )
    for c in copies:
        c.start()
    acc[...] = jnp.zeros_like(acc)
    for c in copies:
        c.wait()
    frame, box, batch, quad = z.frame, z.box, z.batch, z.cells // 4
    rows = lax.broadcasted_iota(i32, (z.rows, z.cells), 0)

    def regrouped():
        return dot(raw[...].astype(bf16), regroup[...])

    for first in range(0, z.own, batch):
        todo = min(batch, z.own - first)
        for i in range(batch):
            for k in range(z.span):
                at = i * frame + k * z.rows
                if i < todo:
                    raw[at : at + z.rows, :] = window[k, mine[0, first + i]].astype(f32)
                else:
                    raw[at : at + z.rows, :] = jnp.zeros((z.rows, z.cells), f32)
        done = regrouped()
        for i in range(todo):
            own[first + i] = done[i * frame : (i + 1) * frame]

    lane_in = lax.broadcasted_iota(i32, (box, batch * frame), 1)
    lane_back = lax.broadcasted_iota(i32, (frame, batch * box), 1)

    def step(b, _):
        first = b * batch
        for i in range(batch):
            color, start = slots[1, first + i], slots[2, first + i]
            for k in range(z.span):
                at = i * frame + k * z.rows
                r = rows + (k * z.rows - start)
                inside = (r >= 0) & (r < box)
                raw[at : at + z.rows, :] = jnp.where(inside, window[k, color].astype(f32), 0.0)
        held[...] = regrouped()
        lhs_in, lhs_back, density = [], [], []
        for i in range(batch):
            m, sub = slots[0, first + i], slots[3, first + i]
            lo = i * frame
            lhs_in.append(jnp.where((lane_in >= lo) & (lane_in < lo + frame), into[sub], 0.0))
            lo = i * box
            lhs_back.append(jnp.where((lane_back >= lo) & (lane_back < lo + box), back[sub], 0.0))
            density.append(own[m] * held[i * frame : (i + 1) * frame])
        x = dot3(split2(jnp.concatenate(lhs_in, 0)), split2(jnp.concatenate(density, 0)))
        q = [x[:, i * quad : (i + 1) * quad] for i in range(4)]
        a, b_, c, d = q[0] + q[2], q[0] - q[2], q[1] + q[3], q[1] - q[3]
        folded = (a + c, a - c, b_ + d, b_ - d)
        solved = []
        for i in range(4):
            y = dot3(split2(folded[i]), (forward[0, i], forward[1, i]))
            factor = scale[:, i * quad : (i + 1) * quad]
            y = (y.reshape(batch, box, quad) * factor[None]).reshape(batch * box, quad)
            solved.append(dot3(split2(y), (backward[0, i], backward[1, i])))
        ee, eo, oe, oo = solved
        a, b_, c, d = ee + oe, ee - oe, eo + oo, eo - oo
        field = jnp.concatenate([a + c, a - c, b_ + d, b_ - d], axis=1)
        v = dot3(split2(jnp.concatenate(lhs_back, 0)), split2(field))
        for i in range(batch):
            m = slots[0, first + i]
            lo = i * frame
            acc[m] = acc[m] + v[lo : lo + frame] * held[lo : lo + frame]
        return 0

    lax.fori_loop(0, (count[0] + batch - 1) // batch, step, 0)
    for m in range(z.own):
        x = acc[m]
        one = x.astype(bf16)
        left = x - one.astype(f32)
        two, three = split2(left)
        res = dot(one, ungroup[...]) + (dot(two, ungroup[...]) + dot(three, ungroup[...]))
        for k in range(z.span):
            outs[k][m] = res[k * z.rows : (k + 1) * z.rows]


def pair_part(z, ids, count, slots, mine, here, pieces):
    tables = pair_tables(z)
    smem = pl.BlockSpec(memory_space=pltpu.SMEM)
    vmem = pl.BlockSpec(memory_space=pltpu.VMEM)
    hbm = pl.BlockSpec(memory_space=pl.ANY)
    names = ("regroup", "ungroup", "forward", "backward", "scale", "into", "back")
    wide = z.batch * z.frame
    return pl.pallas_call(
        functools.partial(pair_kernel, z),
        out_shape=[jax.ShapeDtypeStruct((z.own, z.rows, z.cells), f32)] * z.span,
        in_specs=[smem] * 4 + [hbm] * (1 + len(pieces)) + [vmem] * len(names),
        out_specs=[vmem] * z.span,
        scratch_shapes=[
            pltpu.VMEM((z.span, z.colors, z.rows, z.cells), bf16),
            pltpu.VMEM((wide, z.cells), f32),
            pltpu.VMEM((z.own, z.frame, z.cells), f32),
            pltpu.VMEM((wide, z.cells), f32),
            pltpu.VMEM((z.own, z.frame, z.cells), f32),
            pltpu.SemaphoreType.DMA((1 + len(pieces),)),
        ],
        compiler_params=pltpu.CompilerParams(vmem_limit_bytes=56 << 20),
        cost_estimate=pl.CostEstimate(flops=20_000_000_000, bytes_accessed=16_000_000, transcendentals=0),
        name="pair_solves",
    )(ids, count, slots, mine, here, *pieces, *[jnp.asarray(tables[n]) for n in names])


def local_kernel(z, per_step, ids, shift, here, potential, *rest):
    pieces, rest = rest[: 2 * z.groups], rest[2 * z.groups :]
    plane, along, out, near, lhs, sems = rest
    q, g = ids[0], ids[1]
    order = butterfly_order(z.groups)
    step = pl.program_id(0)

    @pl.when(step == 0)
    def _():
        copies = []
        for s in range(2):
            for p in range(z.groups):
                at = (g ^ order[p]) * z.part
                copies.append(
                    pltpu.make_async_copy(
                        pieces[s * z.groups + p], near.at[s, pl.ds(at, z.part)], sems.at[len(copies)]
                    )
                )
        for c in copies:
            c.start()
        for c in copies:
            c.wait()

    rows, cells, kc = z.rows, z.cells, kin_colors
    lane = lax.broadcasted_iota(i32, (rows, 3 * kc * rows), 1)
    centre = here[...].reshape(per_step * rows, cells)
    tile = 256
    cols = []
    for j in range(0, cells, tile):
        lo, hi = max(0, j - stencil_reach * z.box), min(cells, j + tile + stencil_reach * z.box)
        lo, hi = lo // tile * tile, -(-hi // tile) * tile
        u = centre[:, lo:hi]
        cols.append(dot(u, plane[0, lo:hi, j : j + tile]) + dot(u, plane[1, lo:hi, j : j + tile]))
    flat = jnp.concatenate(cols, axis=1)
    pot = potential[...]
    for s in range(per_step // kc):
        first = step * per_step + s * kc
        for i in range(kc):
            start = lax.rem(shift[first + i] - q * rows + z.grid, z.box)
            lhs[i * rows : (i + 1) * rows, :] = jnp.where(lane // rows % kc == i, along[start], 0.0)
        mid = centre[s * kc * rows : (s + 1) * kc * rows]
        before = near[0, pl.ds(first, kc)].reshape(kc * rows, cells)
        after = near[1, pl.ds(first, kc)].reshape(kc * rows, cells)
        stack = jnp.concatenate([before, mid, after], axis=0)
        head, low = split2(lhs[...])
        kin = dot(head, stack) + dot(low, stack) + flat[s * kc * rows : (s + 1) * kc * rows]
        value = kin.reshape(kc, rows, cells) + pot[None] * mid.astype(f32).reshape(kc, rows, cells)
        out[s * kc : (s + 1) * kc] = value


def local_part(z, ids, shift, here, potential, pieces):
    plane, along = stencil_tables(z)
    per_step = kin_colors * max(d for d in (1, 2, 3, 4) if z.colors // kin_colors % d == 0)
    smem = pl.BlockSpec(memory_space=pltpu.SMEM)
    hbm = pl.BlockSpec(memory_space=pl.ANY)
    block = pl.BlockSpec((per_step, z.rows, z.cells), lambda i: (i, 0, 0))
    vmem = pl.BlockSpec(memory_space=pltpu.VMEM)
    return pl.pallas_call(
        functools.partial(local_kernel, z, per_step),
        grid=(z.colors // per_step,),
        out_shape=jax.ShapeDtypeStruct((z.colors, z.rows, z.cells), f32),
        in_specs=[smem, smem, block, vmem] + [hbm] * len(pieces) + [vmem] * 2,
        out_specs=block,
        scratch_shapes=[
            pltpu.VMEM((2, z.colors, z.rows, z.cells), bf16),
            pltpu.VMEM((kin_colors * z.rows, 3 * kin_colors * z.rows), f32),
            pltpu.SemaphoreType.DMA((len(pieces),)),
        ],
        compiler_params=pltpu.CompilerParams(
            vmem_limit_bytes=40 << 20, dimension_semantics=("arbitrary",)
        ),
        cost_estimate=pl.CostEstimate(flops=6_000_000_000, bytes_accessed=12_000_000, transcendentals=0),
        name="local",
    )(ids, shift, here, potential, *pieces, jnp.asarray(plane), jnp.asarray(along))


def finish_kernel(z, per_step, ids, src, local, *rest):
    pieces, out, gathered, sems = rest[: z.groups], rest[z.groups], rest[z.groups + 1], rest[z.groups + 2]
    order = butterfly_order(z.groups)
    step = pl.program_id(0)
    size = z.width * z.own

    @pl.when(step == 0)
    def _():
        copies = [
            pltpu.make_async_copy(pieces[p], gathered.at[pl.ds((ids[1] ^ order[p]) * size, size)], sems.at[p])
            for p in range(z.groups)
        ]
        for c in copies:
            c.start()
        for c in copies:
            c.wait()

    for i in range(per_step):
        out[i] = local[i] + gathered[src[step * per_step + i]]


def finish(z, ids, src, local, pieces):
    per_step = z.colors // 8 if z.colors % 8 == 0 else 1
    smem = pl.BlockSpec(memory_space=pltpu.SMEM)
    hbm = pl.BlockSpec(memory_space=pl.ANY)
    block = pl.BlockSpec((per_step, z.rows, z.cells), lambda i: (i, 0, 0))
    return pl.pallas_call(
        functools.partial(finish_kernel, z, per_step),
        grid=(z.colors // per_step,),
        out_shape=jax.ShapeDtypeStruct(local.shape, f32),
        in_specs=[smem, smem, block] + [hbm] * len(pieces),
        out_specs=block,
        scratch_shapes=[
            pltpu.VMEM((z.groups * z.width * z.own, z.rows, z.cells), f32),
            pltpu.SemaphoreType.DMA((z.groups,)),
        ],
        compiler_params=pltpu.CompilerParams(
            vmem_limit_bytes=24 << 20, dimension_semantics=("arbitrary",)
        ),
        name="finish",
    )(ids, src, local, *pieces)


def from_slab(x, away, slabs):
    return lax.ppermute(x, "orb", [((i + away) % slabs, i) for i in range(slabs)])


def swapped(x, bit, groups):
    return lax.ppermute(x, "group", [(i, i ^ bit) for i in range(groups)])


def shared(piece, groups):
    have, step = [piece], groups // 2
    while step:
        have += [swapped(x, step, groups) for x in have]
        step //= 2
    return have


def body(orbitals, potential, box_shift, pair_partner, pair_member):
    slabs, groups = lax.axis_size("orb"), lax.axis_size("group")
    z = Sizes(orbitals, pair_partner, groups, slabs)
    q, g = lax.axis_index("orb"), lax.axis_index("group")
    ids = jnp.stack([q, g]).astype(i32)
    mine = lax.dynamic_slice_in_dim(orbitals, g * z.part, z.part, 0)
    pieces = []
    for k in range(z.span):
        if k != z.mid:
            pieces.append(shared(from_slab(mine, k - z.mid, slabs), groups))
    count, slots, home, src = plan(z, ids, box_shift, pair_partner, pair_member)
    local = local_part(
        z, ids, box_shift, orbitals, potential, pieces[z.mid - 1] + pieces[z.mid]
    )
    spread = pair_part(z, ids, count, slots, home, orbitals, [x for p in pieces for x in p])
    parts = [
        spread[k] if k == z.mid else from_slab(spread[k], z.mid - k, slabs) for k in range(z.span)
    ]
    parts = [parts[0] + parts[-1]] + parts[1:-1]
    return finish(z, ids, src, local, shared(jnp.concatenate(parts, axis=0), groups))


def solution(mesh):
    placed = (P(None, "orb", None), P("orb", None), P(), P(), P())
    return jax.shard_map(
        body, mesh=mesh, in_specs=placed, out_specs=P(None, "orb", None), check_vma=False
    )
```

```python
import functools
import math
from typing import NamedTuple

import jax
import jax.numpy as jnp
import numpy as np
from jax import lax
from jax.experimental import pallas as pl
from jax.experimental.pallas import tpu as pltpu
from jax.sharding import PartitionSpec as P

lap_weights = (
    -5369.0 / 1800.0,
    12.0 / 7.0,
    -15.0 / 56.0,
    10.0 / 189.0,
    -1.0 / 112.0,
    2.0 / 1925.0,
    -1.0 / 16632.0,
)
stencil_reach = 6
mixing = 0.25
f32, bf16, i32, i16 = jnp.float32, jnp.bfloat16, jnp.int32, jnp.int16
kin_colors = 8
EMPTY = -(1 << 20)
LANES = 128
TOP = 32767.0
STEPS = 256.0


def split_np(values):
    head = np.asarray(values, np.float32).astype(bf16)
    rest = (values - head.astype(np.float64)).astype(np.float32).astype(bf16)
    return np.stack([head, rest])


def split2(x):
    head = x.astype(bf16)
    return head, (x - head.astype(f32)).astype(bf16)


def dot(a, b):
    return jnp.dot(a, b, preferred_element_type=f32)


def dot3(a, b):
    return dot(a[0], b[0]) + (dot(a[0], b[1]) + dot(a[1], b[0]))


class Sizes:
    def __init__(self, orbitals, pair_partner, groups, slabs):
        self.colors, self.rows, self.cells = orbitals.shape
        self.groups, self.slabs = groups, slabs
        self.box = math.isqrt(self.cells)
        self.width = self.box // self.rows
        self.span = self.width + 1
        self.mid = self.width // 2
        self.home = self.colors // self.width
        self.blocks = pair_partner.shape[0] // slabs
        self.members = self.home // self.blocks
        self.slots = pair_partner.shape[1]
        self.grid = slabs * self.rows
        self.per = self.grid // self.box
        self.part = self.colors // groups
        self.own = self.home // groups
        self.frame = self.span * self.rows
        self.batch = max(1, 256 // self.frame)
        self.planes = self.own + -(-self.own * LANES // self.cells)
        self.cap = -(-self.blocks * self.slots // self.batch) * self.batch + self.batch


def butterfly_order(groups):
    order, step = [0], groups // 2
    while step:
        order += [o ^ step for o in order]
        step //= 2
    return order


def sine_matrix(box):
    count = np.arange(1, box + 1)
    return np.sqrt(2.0 / (box + 1)) * np.sin(np.pi * np.outer(count, count) / (box + 1))


def pair_tables(z):
    box, half = z.box, z.box // 2
    sine = sine_matrix(box)
    side = [np.arange(half), box - 1 - np.arange(half)]
    order = np.concatenate([(y[:, None] * box + x[None, :]).reshape(-1) for y in side for x in side])
    regroup = np.zeros((z.cells, z.cells))
    regroup[order, np.arange(z.cells)] = 1.0
    halves = [sine[0::2, :half], sine[1::2, :half]]
    forward = np.stack([np.kron(a, b).T for a in halves for b in halves])
    backward = np.stack([m.T for m in forward])
    single = 2.0 - 2.0 * np.cos(np.pi * np.arange(1, box + 1) / (box + 1))
    modes = [(single[py::2][:, None] + single[pz::2][None, :]).reshape(-1) for py in (0, 1) for pz in (0, 1)]
    scale = -mixing / (single[:, None] + np.concatenate(modes)[None, :])
    into = np.zeros((z.rows, box, z.batch * z.frame))
    back = np.zeros((z.rows, z.frame, z.batch * box))
    for sub in range(z.rows):
        for i in range(z.batch):
            into[sub, :, i * z.frame + sub : i * z.frame + sub + box] = sine
            back[sub, sub : sub + box, i * box : (i + 1) * box] = sine.T
    return dict(
        regroup=regroup.astype(bf16),
        ungroup=regroup.T.astype(bf16),
        forward=split_np(forward),
        backward=split_np(backward),
        scale=scale.astype(np.float32),
        into=into.astype(np.float32),
        back=back.astype(np.float32),
    )


def stencil_tables(z):
    box, rows = z.box, z.rows
    band = np.zeros((box, box))
    for off in range(1, stencil_reach + 1):
        band += lap_weights[off] * (np.eye(box, k=off) + np.eye(box, k=-off))
    eye = np.eye(box)
    plane = -0.5 * (3.0 * lap_weights[0] * np.eye(z.cells) + np.kron(band, eye) + np.kron(eye, band))
    along = np.zeros((box, rows, 3 * kin_colors * rows))
    for start in range(box):
        for x in range(rows):
            for y in range(-rows, 2 * rows):
                off = abs(y - x)
                if off and off <= stencil_reach and (x - start) // box == (y - start) // box:
                    for i in range(kin_colors):
                        at = ((y + rows) // rows) * kin_colors * rows + i * rows + y % rows
                        along[start, x, at] = -0.5 * lap_weights[off]
    return split_np(plane), along.astype(np.float32)


def plan_kernel(z, ids, shift, partner, member, count_ref, slot_ref, mine_ref, src_ref, order, filled):
    q, g = ids[0], ids[1]
    o = lax.rem(q + z.slabs - z.mid, z.slabs)
    for c in range(z.width):
        filled[c] = 0

    def color_step(c, _):
        cls = shift[c] // z.rows
        n = filled[cls]
        filled[cls] = n + 1
        order[cls, n] = c
        back = lax.rem(q - cls + z.slabs * z.width, z.width)
        src_ref[0, c] = (lax.rem(n, z.groups) * z.width + back) * z.planes
        src_ref[1, c] = n // z.groups
        return 0

    lax.fori_loop(0, z.colors, color_step, 0)
    home_class = lax.rem(o, z.width)
    for m in range(z.own):
        c = order[home_class, m * z.groups + g]
        mine_ref[0, m] = c
        mine_ref[1, m] = lax.rem(shift[c], z.rows)
    total = jnp.int32(0)
    for t in range(z.blocks):

        def slot_step(p, total, t=t):
            j = partner[o * z.blocks + t, p]
            n = t * z.members + member[o * z.blocks + t, p]
            live = jnp.logical_and(j >= 0, lax.rem(n, z.groups) == g)
            j = jnp.maximum(j, 0)
            cj = j // z.per
            sub = lax.rem(shift[order[home_class, n]], z.rows)
            there = (j - cj * z.per) * z.box + shift[cj]
            d = there - (o * z.rows + sub) + z.grid // 2
            d = lax.rem(d + z.grid, z.grid) - z.grid // 2
            slot_ref[0, total] = n // z.groups
            slot_ref[1, total] = cj
            slot_ref[2, total] = sub + d
            slot_ref[3, total] = sub
            return total + live.astype(i32)

        total = lax.fori_loop(0, z.slots, slot_step, total)
    count_ref[0] = total
    for i in range(z.batch):
        slot_ref[0, total + i] = 0
        slot_ref[1, total + i] = 0
        slot_ref[2, total + i] = EMPTY
        slot_ref[3, total + i] = 0


def plan(z, ids, shift, partner, member):
    smem = pl.BlockSpec(memory_space=pltpu.SMEM)
    return pl.pallas_call(
        functools.partial(plan_kernel, z),
        out_shape=(
            jax.ShapeDtypeStruct((1,), i32),
            jax.ShapeDtypeStruct((4, z.cap), i32),
            jax.ShapeDtypeStruct((2, z.own), i32),
            jax.ShapeDtypeStruct((2, z.colors), i32),
        ),
        in_specs=[smem] * 4,
        out_specs=(smem,) * 4,
        scratch_shapes=[pltpu.SMEM((z.width, z.colors), i32), pltpu.SMEM((z.width,), i32)],
        cost_estimate=pl.CostEstimate(flops=10_000_000_000, bytes_accessed=100_000, transcendentals=0),
        name="plan",
    )(ids, shift, partner, member)


class Piece(NamedTuple):
    even: int
    odd: int
    flip: int
    parts: int
    unit: int
    add: int
    size: int

    def slab(self, q):
        return jnp.where(lax.rem(q, 2) == 0, self.even, self.odd)

    def colors(self, g):
        return pl.ds(lax.rem(g ^ self.flip, self.parts) * self.unit + self.add, self.size)


def scale_of(code):
    return jnp.exp2(code.astype(f32) * (1.0 / STEPS)) * (1.0 / TOP)


def coded(x):
    groups = [x[:, i : i + LANES] for i in range(0, x.shape[1], LANES)]
    top = functools.reduce(jnp.maximum, [jnp.abs(v) for v in groups])
    code = jnp.ceil(jnp.log2(jnp.clip(top, 2.0**-100, 2.0**100)) * STEPS) + 1.0
    factor = 1.0 / scale_of(code)
    whole = [jnp.clip(jnp.round(v * factor), -TOP, TOP).astype(i32) for v in groups]
    return jnp.concatenate(whole, axis=1), jnp.where(top > 0, code, 0.0).astype(i32)


def pair_kernel(z, layout, ids, count, slots, mine, here, *rest):
    pieces, rest = rest[: len(layout)], rest[len(layout) :]
    (regroup, ungroup, forward, backward, scale, into, back), rest = rest[:7], rest[7:]
    outs, rest = rest[: z.span], rest[z.span :]
    window, raw, own, held, acc, sems = rest
    q, g = ids[0], ids[1]
    copies = [pltpu.make_async_copy(here, window.at[z.mid], sems.at[0])]
    for piece, ref in zip(layout, pieces):
        to = window.at[piece.slab(q), piece.colors(g)]
        copies.append(pltpu.make_async_copy(ref, to, sems.at[len(copies)]))
    for c in copies:
        c.start()
    acc[...] = jnp.zeros_like(acc)
    for c in copies:
        c.wait()
    frame, box, batch, quad = z.frame, z.box, z.batch, z.cells // 4
    rows = lax.broadcasted_iota(i32, (z.rows, z.cells), 0)

    def regrouped():
        return dot(raw[...].astype(bf16), regroup[...])

    for first in range(0, z.own, batch):
        todo = min(batch, z.own - first)
        for i in range(batch):
            for k in range(z.span):
                at = i * frame + k * z.rows
                if i < todo:
                    raw[at : at + z.rows, :] = window[k, mine[0, first + i]].astype(f32)
                else:
                    raw[at : at + z.rows, :] = jnp.zeros((z.rows, z.cells), f32)
        done = regrouped()
        for i in range(todo):
            own[first + i] = done[i * frame : (i + 1) * frame]

    lane_in = lax.broadcasted_iota(i32, (box, batch * frame), 1)
    lane_back = lax.broadcasted_iota(i32, (frame, batch * box), 1)

    def step(b, _):
        first = b * batch
        for i in range(batch):
            color, start = slots[1, first + i], slots[2, first + i]
            for k in range(z.span):
                at = i * frame + k * z.rows
                r = rows + (k * z.rows - start)
                inside = (r >= 0) & (r < box)
                raw[at : at + z.rows, :] = jnp.where(inside, window[k, color].astype(f32), 0.0)
        held[...] = regrouped()
        lhs_in, lhs_back, density = [], [], []
        for i in range(batch):
            m, sub = slots[0, first + i], slots[3, first + i]
            lo = i * frame
            lhs_in.append(jnp.where((lane_in >= lo) & (lane_in < lo + frame), into[sub], 0.0))
            lo = i * box
            lhs_back.append(jnp.where((lane_back >= lo) & (lane_back < lo + box), back[sub], 0.0))
            density.append(own[m] * held[i * frame : (i + 1) * frame])
        x = dot3(split2(jnp.concatenate(lhs_in, 0)), split2(jnp.concatenate(density, 0)))
        q = [x[:, i * quad : (i + 1) * quad] for i in range(4)]
        a, b_, c, d = q[0] + q[2], q[0] - q[2], q[1] + q[3], q[1] - q[3]
        folded = (a + c, a - c, b_ + d, b_ - d)
        solved = []
        for i in range(4):
            y = dot3(split2(folded[i]), (forward[0, i], forward[1, i]))
            factor = scale[:, i * quad : (i + 1) * quad]
            y = (y.reshape(batch, box, quad) * factor[None]).reshape(batch * box, quad)
            solved.append(dot3(split2(y), (backward[0, i], backward[1, i])))
        ee, eo, oe, oo = solved
        a, b_, c, d = ee + oe, ee - oe, eo + oo, eo - oo
        field = jnp.concatenate([a + c, a - c, b_ + d, b_ - d], axis=1)
        v = dot3(split2(jnp.concatenate(lhs_back, 0)), split2(field))
        for i in range(batch):
            at = pl.ds(slots[0, first + i] * frame, frame)
            lo = i * frame
            acc[at, :] = acc[at, :] + v[lo : lo + frame] * held[lo : lo + frame]
        return 0

    lax.fori_loop(0, (count[0] + batch - 1) // batch, step, 0)
    head, low = split2(acc[...])
    res = dot(head, ungroup[...]) + dot(low, ungroup[...])
    values, codes = coded(res)
    for m in range(z.own):
        for k in range(z.span):
            at = m * frame + k * z.rows
            outs[k][m] = values[at : at + z.rows].astype(i16)
            plane, lane = z.own + m * LANES // z.cells, m * LANES % z.cells
            outs[k][plane, :, lane : lane + LANES] = codes[at : at + z.rows].astype(i16)


def pair_part(z, ids, count, slots, mine, here, layout, pieces):
    tables = pair_tables(z)
    smem = pl.BlockSpec(memory_space=pltpu.SMEM)
    vmem = pl.BlockSpec(memory_space=pltpu.VMEM)
    hbm = pl.BlockSpec(memory_space=pl.ANY)
    names = ("regroup", "ungroup", "forward", "backward", "scale", "into", "back")
    wide = z.batch * z.frame
    return pl.pallas_call(
        functools.partial(pair_kernel, z, layout),
        out_shape=[jax.ShapeDtypeStruct((z.planes, z.rows, z.cells), i16)] * z.span,
        in_specs=[smem] * 4 + [hbm] * (1 + len(pieces)) + [vmem] * len(names),
        out_specs=[vmem] * z.span,
        scratch_shapes=[
            pltpu.VMEM((z.span, z.colors, z.rows, z.cells), bf16),
            pltpu.VMEM((wide, z.cells), f32),
            pltpu.VMEM((z.own, z.frame, z.cells), f32),
            pltpu.VMEM((wide, z.cells), f32),
            pltpu.VMEM((z.own * z.frame, z.cells), f32),
            pltpu.SemaphoreType.DMA((1 + len(pieces),)),
        ],
        compiler_params=pltpu.CompilerParams(vmem_limit_bytes=34 << 20),
        cost_estimate=pl.CostEstimate(flops=20_000_000_000, bytes_accessed=16_000_000, transcendentals=0),
        name="pair_solves",
    )(ids, count, slots, mine, here, *pieces, *[jnp.asarray(tables[n]) for n in names])


def plane_kernel(z, per_step, here, potential, plane, out):
    centre = here[...].reshape(per_step * z.rows, z.cells)
    tile, reach = 256, stencil_reach * z.box
    cols = []
    for j in range(0, z.cells, tile):
        lo, hi = max(0, j - reach) // tile * tile, -(-min(z.cells, j + tile + reach) // tile) * tile
        u = centre[:, lo:hi]
        cols.append(dot(u, plane[0, lo:hi, j : j + tile]) + dot(u, plane[1, lo:hi, j : j + tile]))
    flat = jnp.concatenate(cols, axis=1).reshape(per_step, z.rows, z.cells)
    out[...] = flat + potential[...][None] * here[...].astype(f32)


def plane_part(z, here, potential, plane):
    per_step = kin_colors * max(d for d in (1, 2, 3, 4) if z.colors // kin_colors % d == 0)
    block = pl.BlockSpec((per_step, z.rows, z.cells), lambda i: (i, 0, 0))
    vmem = pl.BlockSpec(memory_space=pltpu.VMEM)
    return pl.pallas_call(
        functools.partial(plane_kernel, z, per_step),
        grid=(z.colors // per_step,),
        out_shape=jax.ShapeDtypeStruct((z.colors, z.rows, z.cells), f32),
        in_specs=[block, vmem, vmem],
        out_specs=block,
        compiler_params=pltpu.CompilerParams(
            vmem_limit_bytes=16 << 20, dimension_semantics=("arbitrary",)
        ),
        cost_estimate=pl.CostEstimate(flops=6_000_000_000, bytes_accessed=12_000_000, transcendentals=0),
        name="plane",
    )(here, potential, plane)


def along_kernel(z, per_step, layout, ids, shift, here, flat, *rest):
    pieces, rest = rest[: len(layout)], rest[len(layout) :]
    along, out, near, lhs, sems = rest
    q, g = ids[0], ids[1]
    step = pl.program_id(0)

    @pl.when(step == 0)
    def _():
        copies = []
        for piece, ref in zip(layout, pieces):
            to = near.at[(piece.slab(q) > z.mid).astype(i32), piece.colors(g)]
            copies.append(pltpu.make_async_copy(ref, to, sems.at[len(copies)]))
        for c in copies:
            c.start()
        for c in copies:
            c.wait()

    rows, cells, kc = z.rows, z.cells, kin_colors
    lane = lax.broadcasted_iota(i32, (rows, 3 * kc * rows), 1)
    for s in range(per_step // kc):
        first = step * per_step + s * kc
        for i in range(kc):
            start = lax.rem(shift[first + i] - q * rows + z.grid, z.box)
            lhs[i * rows : (i + 1) * rows, :] = jnp.where(lane // rows % kc == i, along[start], 0.0)
        mid = here[s * kc : (s + 1) * kc].reshape(kc * rows, cells)
        before = near[0, pl.ds(first, kc)].reshape(kc * rows, cells)
        after = near[1, pl.ds(first, kc)].reshape(kc * rows, cells)
        stack = jnp.concatenate([before, mid, after], axis=0)
        head, low = split2(lhs[...])
        kin = (dot(head, stack) + dot(low, stack)).reshape(kc, rows, cells)
        out[s * kc : (s + 1) * kc] = flat[s * kc : (s + 1) * kc] + kin


def along_part(z, ids, shift, here, flat, layout, pieces, along):
    per_step = kin_colors * max(d for d in (1, 2, 3, 4) if z.colors // kin_colors % d == 0)
    smem = pl.BlockSpec(memory_space=pltpu.SMEM)
    hbm = pl.BlockSpec(memory_space=pl.ANY)
    block = pl.BlockSpec((per_step, z.rows, z.cells), lambda i: (i, 0, 0))
    vmem = pl.BlockSpec(memory_space=pltpu.VMEM)
    return pl.pallas_call(
        functools.partial(along_kernel, z, per_step, layout),
        grid=(z.colors // per_step,),
        out_shape=jax.ShapeDtypeStruct((z.colors, z.rows, z.cells), f32),
        in_specs=[smem, smem, block, block] + [hbm] * len(pieces) + [vmem],
        out_specs=block,
        scratch_shapes=[
            pltpu.VMEM((2, z.colors, z.rows, z.cells), bf16),
            pltpu.VMEM((kin_colors * z.rows, 3 * kin_colors * z.rows), f32),
            pltpu.SemaphoreType.DMA((len(pieces),)),
        ],
        compiler_params=pltpu.CompilerParams(
            vmem_limit_bytes=16 << 20, dimension_semantics=("arbitrary",)
        ),
        cost_estimate=pl.CostEstimate(flops=5_000_000_000, bytes_accessed=12_000_000, transcendentals=0),
        name="along",
    )(ids, shift, here, flat, *pieces, along)


def finish_kernel(z, per_step, ids, src, local, *rest):
    pieces, out, gathered, sems = rest[: z.groups], rest[z.groups], rest[z.groups + 1], rest[z.groups + 2]
    order = butterfly_order(z.groups)
    step = pl.program_id(0)
    size = z.width * z.planes

    @pl.when(step == 0)
    def _():
        copies = [
            pltpu.make_async_copy(pieces[p], gathered.at[pl.ds((ids[1] ^ order[p]) * size, size)], sems.at[p])
            for p in range(z.groups)
        ]
        for c in copies:
            c.start()
        for c in copies:
            c.wait()

    for i in range(per_step):
        first, m = src[0, step * per_step + i], src[1, step * per_step + i]
        at = m * LANES
        lane = pl.multiple_of(lax.rem(at, z.cells), LANES)
        scale = scale_of(gathered[first + z.own + at // z.cells, :, pl.ds(lane, LANES)])
        value = gathered[first + m].astype(f32)
        out[i] = local[i] + value * jnp.concatenate([scale] * (z.cells // LANES), axis=1)


def finish(z, ids, src, local, pieces):
    per_step = z.colors // 8 if z.colors % 8 == 0 else 1
    smem = pl.BlockSpec(memory_space=pltpu.SMEM)
    hbm = pl.BlockSpec(memory_space=pl.ANY)
    block = pl.BlockSpec((per_step, z.rows, z.cells), lambda i: (i, 0, 0))
    return pl.pallas_call(
        functools.partial(finish_kernel, z, per_step),
        grid=(z.colors // per_step,),
        out_shape=jax.ShapeDtypeStruct(local.shape, f32),
        in_specs=[smem, smem, block] + [hbm] * len(pieces),
        out_specs=block,
        scratch_shapes=[
            pltpu.VMEM((z.groups * z.width * z.planes, z.rows, z.cells), i16),
            pltpu.SemaphoreType.DMA((z.groups,)),
        ],
        compiler_params=pltpu.CompilerParams(
            vmem_limit_bytes=12 << 20, dimension_semantics=("arbitrary",)
        ),
        name="finish",
    )(ids, src, local, *pieces)


def moved(x, source, slabs):
    return lax.ppermute(x, "orb", [(source(i) % slabs, i) for i in range(slabs)])


def from_slab(x, away, slabs):
    return moved(x, lambda i: i + away, slabs)


def swapped(x, bit, groups):
    return lax.ppermute(x, "group", [(i, i ^ bit) for i in range(groups)])


def shared(piece, groups):
    have, step = [piece], groups // 2
    while step:
        have += [swapped(x, step, groups) for x in have]
        step //= 2
    return have


def after(x, *others):
    return lax.optimization_barrier((x, *others))[0]


def fetch(z, orbitals, g, early_work, late_work):
    quarter = lax.dynamic_slice_in_dim(orbitals, g * z.part, z.part, 0)
    slabs, groups = z.slabs, z.groups
    layout, pieces = [], []

    def keep(even, odd, flips, have):
        for flip, x in zip(flips, have):
            layout.append(Piece(even, odd, flip, groups, z.part, 0, z.part))
            pieces.append(x)

    quarters = butterfly_order(groups)
    if z.mid != 2 or slabs % 2 or groups < 2:
        done = *early_work(), late_work()
        for k in range(z.span):
            if k != z.mid:
                keep(k, k, quarters, shared(from_slab(quarter, k - z.mid, slabs), groups))
        return layout, pieces, done
    half, lo, hi = z.colors // 2, z.mid - 2, z.mid + 2
    chunk = half // 2
    firsts = [
        lax.dynamic_slice_in_dim(orbitals, lax.rem(g, 2) * half + i * chunk, chunk, 0) for i in range(2)
    ]
    side = [moved(x, lambda i: i + 2 if i % 2 == 0 else i - 2, slabs) for x in firsts]
    near = moved(quarter, lambda i: i ^ 1, slabs)
    rest = moved(quarter, lambda i: i - 2 if i % 2 == 0 else i + 2, slabs)
    done = early_work()
    flat = late_work()
    side = [after(x, *done, flat) for x in side]
    far = [moved(x, lambda i: i ^ 1, slabs) for x in side]
    keep(lo + 3, lo + 1, quarters, shared(after(near, *done, flat), groups))
    for i in range(2):
        for x, even, odd in ((side[i], hi, lo), (far[i], lo + 1, lo + 3)):
            for flip, y in enumerate((x, swapped(x, 1, groups))):
                layout.append(Piece(even, odd, flip, 2, half, i * chunk, chunk))
                pieces.append(y)
    keep(lo, hi, quarters, shared(after(rest, flat), groups))
    return layout, pieces, (*done, flat)


def body(orbitals, potential, box_shift, pair_partner, pair_member):
    slabs, groups = lax.axis_size("orb"), lax.axis_size("group")
    z = Sizes(orbitals, pair_partner, groups, slabs)
    q, g = lax.axis_index("orb"), lax.axis_index("group")
    ids = jnp.stack([q, g]).astype(i32)
    plane, along = [jnp.asarray(t) for t in stencil_tables(z)]
    layout, pieces, done = fetch(
        z,
        orbitals,
        g,
        lambda: plan(z, ids, box_shift, pair_partner, pair_member),
        lambda: plane_part(z, orbitals, potential, plane),
    )
    count, slots, home, src, flat = done
    beside = [i for i, p in enumerate(layout) if {p.even, p.odd} <= {z.mid - 1, z.mid + 1}]
    local = along_part(
        z, ids, box_shift, orbitals, flat, [layout[i] for i in beside], [pieces[i] for i in beside], along
    )
    spread = pair_part(z, ids, count, slots, home, orbitals, layout, pieces)
    parts = [
        spread[k] if k == z.mid else from_slab(spread[k], z.mid - k, slabs) for k in range(z.span)
    ]
    parts = [parts[0] + parts[-1]] + parts[1:-1]
    joined = after(jnp.concatenate(parts, axis=0), local)
    return finish(z, ids, src, local, shared(joined, groups))


def solution(mesh):
    placed = (P(None, "orb", None), P("orb", None), P(), P(), P())
    return jax.shard_map(
        body, mesh=mesh, in_specs=placed, out_specs=P(None, "orb", None), check_vma=False
    )
```

```python
import functools
import math
from typing import NamedTuple

import jax
import jax.numpy as jnp
import numpy as np
from jax import lax
from jax.experimental import pallas as pl
from jax.experimental.pallas import tpu as pltpu
from jax.sharding import PartitionSpec as P

lap_weights = (
    -5369.0 / 1800.0,
    12.0 / 7.0,
    -15.0 / 56.0,
    10.0 / 189.0,
    -1.0 / 112.0,
    2.0 / 1925.0,
    -1.0 / 16632.0,
)
stencil_reach = 6
mixing = 0.25
f32, bf16, i32, i16 = jnp.float32, jnp.bfloat16, jnp.int32, jnp.int16
kin_colors = 8
EMPTY = -(1 << 20)
LANES = 128
TOP = 32767.0
STEPS = 256.0


def split_np(values):
    head = np.asarray(values, np.float32).astype(bf16)
    rest = (values - head.astype(np.float64)).astype(np.float32).astype(bf16)
    return np.stack([head, rest])


def split2(x):
    head = x.astype(bf16)
    return head, (x - head.astype(f32)).astype(bf16)


def dot(a, b):
    return jnp.dot(a, b, preferred_element_type=f32)


def dot3(a, b):
    rows = a[0].shape[0]
    both = dot(jnp.concatenate(a, axis=0), b[0])
    return both[:rows] + (dot(a[0], b[1]) + both[rows:])


class Sizes:
    def __init__(self, orbitals, pair_partner, groups, slabs):
        self.colors, self.rows, self.cells = orbitals.shape
        self.groups, self.slabs = groups, slabs
        self.box = math.isqrt(self.cells)
        self.width = self.box // self.rows
        self.span = self.width + 1
        self.mid = self.width // 2
        self.home = self.colors // self.width
        self.blocks = pair_partner.shape[0] // slabs
        self.members = self.home // self.blocks
        self.slots = pair_partner.shape[1]
        self.grid = slabs * self.rows
        self.per = self.grid // self.box
        self.part = self.colors // groups
        self.own = self.home // groups
        self.frame = self.span * self.rows
        self.batch = max(1, 256 // self.frame)
        self.planes = self.own + -(-self.own * LANES // self.cells)
        self.cap = -(-self.blocks * self.slots // self.batch) * self.batch + self.batch


def butterfly_order(groups):
    order, step = [0], groups // 2
    while step:
        order += [o ^ step for o in order]
        step //= 2
    return order


def sine_matrix(box):
    count = np.arange(1, box + 1)
    return np.sqrt(2.0 / (box + 1)) * np.sin(np.pi * np.outer(count, count) / (box + 1))


def pair_tables(z):
    box, half = z.box, z.box // 2
    sine = sine_matrix(box)
    side = [np.arange(half), box - 1 - np.arange(half)]
    order = np.concatenate([(y[:, None] * box + x[None, :]).reshape(-1) for y in side for x in side])
    regroup = np.zeros((z.cells, z.cells))
    regroup[order, np.arange(z.cells)] = 1.0
    halves = [sine[0::2, :half], sine[1::2, :half]]
    forward = np.stack([np.kron(a, b).T for a in halves for b in halves])
    backward = np.stack([m.T for m in forward])
    single = 2.0 - 2.0 * np.cos(np.pi * np.arange(1, box + 1) / (box + 1))
    modes = [(single[py::2][:, None] + single[pz::2][None, :]).reshape(-1) for py in (0, 1) for pz in (0, 1)]
    scale = -mixing / (single[:, None] + np.concatenate(modes)[None, :])
    into = np.zeros((z.rows, box, z.batch * z.frame))
    back = np.zeros((z.rows, z.frame, z.batch * box))
    for sub in range(z.rows):
        for i in range(z.batch):
            into[sub, :, i * z.frame + sub : i * z.frame + sub + box] = sine
            back[sub, sub : sub + box, i * box : (i + 1) * box] = sine.T
    return dict(
        regroup=regroup.astype(bf16),
        ungroup=regroup.T.astype(bf16),
        forward=split_np(forward),
        backward=split_np(backward),
        scale=scale.astype(np.float32),
        into=into.astype(np.float32),
        back=back.astype(np.float32),
    )


def stencil_tables(z):
    box, rows = z.box, z.rows
    band = np.zeros((box, box))
    for off in range(1, stencil_reach + 1):
        band += lap_weights[off] * (np.eye(box, k=off) + np.eye(box, k=-off))
    eye = np.eye(box)
    plane = -0.5 * (3.0 * lap_weights[0] * np.eye(z.cells) + np.kron(band, eye) + np.kron(eye, band))
    along = np.zeros((box, rows, 3 * kin_colors * rows))
    for start in range(box):
        for x in range(rows):
            for y in range(-rows, 2 * rows):
                off = abs(y - x)
                if off and off <= stencil_reach and (x - start) // box == (y - start) // box:
                    for i in range(kin_colors):
                        at = ((y + rows) // rows) * kin_colors * rows + i * rows + y % rows
                        along[start, x, at] = -0.5 * lap_weights[off]
    return split_np(plane), along.astype(np.float32)


def plan_kernel(z, ids, shift, partner, member, count_ref, slot_ref, mine_ref, dst_ref, order, filled):
    q, g = ids[0], ids[1]
    o = lax.rem(q + z.slabs - z.mid, z.slabs)
    for c in range(z.width):
        filled[c] = 0

    def color_step(c, _):
        cls = shift[c] // z.rows
        n = filled[cls]
        filled[cls] = n + 1
        order[cls, n] = c
        back = lax.rem(q - cls + z.slabs * z.width, z.width)
        dst_ref[(lax.rem(n, z.groups) * z.width + back) * z.own + n // z.groups] = c
        return 0

    lax.fori_loop(0, z.colors, color_step, 0)
    home_class = lax.rem(o, z.width)
    for m in range(z.own):
        c = order[home_class, m * z.groups + g]
        mine_ref[0, m] = c
        mine_ref[1, m] = lax.rem(shift[c], z.rows)
    total = jnp.int32(0)
    for t in range(z.blocks):

        def slot_step(p, total, t=t):
            j = partner[o * z.blocks + t, p]
            n = t * z.members + member[o * z.blocks + t, p]
            live = jnp.logical_and(j >= 0, lax.rem(n, z.groups) == g)
            j = jnp.maximum(j, 0)
            cj = j // z.per
            sub = lax.rem(shift[order[home_class, n]], z.rows)
            there = (j - cj * z.per) * z.box + shift[cj]
            d = there - (o * z.rows + sub) + z.grid // 2
            d = lax.rem(d + z.grid, z.grid) - z.grid // 2
            slot_ref[0, total] = n // z.groups
            slot_ref[1, total] = cj
            slot_ref[2, total] = sub + d
            slot_ref[3, total] = sub
            return total + live.astype(i32)

        total = lax.fori_loop(0, z.slots, slot_step, total)
    count_ref[0] = total
    for i in range(z.batch):
        slot_ref[0, total + i] = 0
        slot_ref[1, total + i] = 0
        slot_ref[2, total + i] = EMPTY
        slot_ref[3, total + i] = 0


def plan(z, ids, shift, partner, member):
    smem = pl.BlockSpec(memory_space=pltpu.SMEM)
    return pl.pallas_call(
        functools.partial(plan_kernel, z),
        out_shape=(
            jax.ShapeDtypeStruct((1,), i32),
            jax.ShapeDtypeStruct((4, z.cap), i32),
            jax.ShapeDtypeStruct((2, z.own), i32),
            jax.ShapeDtypeStruct((z.colors,), i32),
        ),
        in_specs=[smem] * 4,
        out_specs=(smem,) * 4,
        scratch_shapes=[pltpu.SMEM((z.width, z.colors), i32), pltpu.SMEM((z.width,), i32)],
        cost_estimate=pl.CostEstimate(flops=10_000_000_000, bytes_accessed=100_000, transcendentals=0),
        name="plan",
    )(ids, shift, partner, member)


class Piece(NamedTuple):
    even: int
    odd: int
    flip: int
    parts: int
    unit: int
    add: int
    size: int

    def slab(self, q):
        return jnp.where(lax.rem(q, 2) == 0, self.even, self.odd)

    def colors(self, g):
        return pl.ds(lax.rem(g ^ self.flip, self.parts) * self.unit + self.add, self.size)


def scale_of(code):
    return jnp.exp2(code.astype(f32) * (1.0 / STEPS)) * (1.0 / TOP)


def coded(x):
    groups = [x[:, i : i + LANES] for i in range(0, x.shape[1], LANES)]
    top = functools.reduce(jnp.maximum, [jnp.abs(v) for v in groups])
    code = jnp.ceil(jnp.log2(jnp.clip(top, 2.0**-100, 2.0**100)) * STEPS) + 1.0
    factor = 1.0 / scale_of(code)
    whole = [jnp.clip(jnp.round(v * factor), -TOP, TOP).astype(i32) for v in groups]
    return jnp.concatenate(whole, axis=1), jnp.where(top > 0, code, 0.0).astype(i32)


def pair_kernel(z, layout, ids, count, slots, mine, here, *rest):
    pieces, rest = rest[: len(layout)], rest[len(layout) :]
    (regroup, ungroup, forward, backward, scale, into, back), rest = rest[:7], rest[7:]
    outs, rest = rest[: z.span], rest[z.span :]
    window, raw, own, held, acc, sems = rest
    q, g = ids[0], ids[1]
    copies = [pltpu.make_async_copy(here, window.at[z.mid], sems.at[0])]
    for piece, ref in zip(layout, pieces):
        to = window.at[piece.slab(q), piece.colors(g)]
        copies.append(pltpu.make_async_copy(ref, to, sems.at[len(copies)]))
    for c in copies:
        c.start()
    acc[...] = jnp.zeros_like(acc)
    for c in copies:
        c.wait()
    frame, box, batch, quad = z.frame, z.box, z.batch, z.cells // 4
    rows = lax.broadcasted_iota(i32, (z.rows, z.cells), 0)

    def regrouped():
        return dot(raw[...].astype(bf16), regroup[...])

    for first in range(0, z.own, batch):
        todo = min(batch, z.own - first)
        for i in range(batch):
            for k in range(z.span):
                at = i * frame + k * z.rows
                if i < todo:
                    raw[at : at + z.rows, :] = window[k, mine[0, first + i]].astype(f32)
                else:
                    raw[at : at + z.rows, :] = jnp.zeros((z.rows, z.cells), f32)
        done = regrouped()
        for i in range(todo):
            own[first + i] = done[i * frame : (i + 1) * frame]

    lane_in = lax.broadcasted_iota(i32, (box, batch * frame), 1)
    lane_back = lax.broadcasted_iota(i32, (frame, batch * box), 1)

    def step(b, _):
        first = b * batch
        for i in range(batch):
            color, start = slots[1, first + i], slots[2, first + i]
            for k in range(z.span):
                at = i * frame + k * z.rows
                r = rows + (k * z.rows - start)
                inside = (r >= 0) & (r < box)
                raw[at : at + z.rows, :] = jnp.where(inside, window[k, color].astype(f32), 0.0)
        held[...] = regrouped()
        lhs_in, lhs_back, density = [], [], []
        for i in range(batch):
            m, sub = slots[0, first + i], slots[3, first + i]
            lo = i * frame
            lhs_in.append(jnp.where((lane_in >= lo) & (lane_in < lo + frame), into[sub], 0.0))
            lo = i * box
            lhs_back.append(jnp.where((lane_back >= lo) & (lane_back < lo + box), back[sub], 0.0))
            density.append(own[m] * held[i * frame : (i + 1) * frame])
        x = dot3(split2(jnp.concatenate(lhs_in, 0)), split2(jnp.concatenate(density, 0)))
        q = [x[:, i * quad : (i + 1) * quad] for i in range(4)]
        a, b_, c, d = q[0] + q[2], q[0] - q[2], q[1] + q[3], q[1] - q[3]
        folded = (a + c, a - c, b_ + d, b_ - d)
        solved = []
        for i in range(4):
            y = dot3(split2(folded[i]), (forward[0, i], forward[1, i]))
            factor = scale[:, i * quad : (i + 1) * quad]
            y = (y.reshape(batch, box, quad) * factor[None]).reshape(batch * box, quad)
            solved.append(dot3(split2(y), (backward[0, i], backward[1, i])))
        ee, eo, oe, oo = solved
        a, b_, c, d = ee + oe, ee - oe, eo + oo, eo - oo
        field = jnp.concatenate([a + c, a - c, b_ + d, b_ - d], axis=1)
        v = dot3(split2(jnp.concatenate(lhs_back, 0)), split2(field))
        for i in range(batch):
            at = pl.ds(slots[0, first + i] * frame, frame)
            lo = i * frame
            acc[at, :] = acc[at, :] + v[lo : lo + frame] * held[lo : lo + frame]
        return 0

    lax.fori_loop(0, (count[0] + batch - 1) // batch, step, 0)
    head, low = split2(acc[...])
    res = dot(head, ungroup[...]) + dot(low, ungroup[...])
    values, codes = coded(res)
    for m in range(z.own):
        for k in range(z.span):
            at = m * frame + k * z.rows
            outs[k][m] = values[at : at + z.rows].astype(i16)
            plane, lane = z.own + m * LANES // z.cells, m * LANES % z.cells
            outs[k][plane, :, lane : lane + LANES] = codes[at : at + z.rows].astype(i16)


def pair_part(z, ids, count, slots, mine, here, layout, pieces):
    tables = pair_tables(z)
    smem = pl.BlockSpec(memory_space=pltpu.SMEM)
    vmem = pl.BlockSpec(memory_space=pltpu.VMEM)
    hbm = pl.BlockSpec(memory_space=pl.ANY)
    names = ("regroup", "ungroup", "forward", "backward", "scale", "into", "back")
    wide = z.batch * z.frame
    return pl.pallas_call(
        functools.partial(pair_kernel, z, layout),
        out_shape=[jax.ShapeDtypeStruct((z.planes, z.rows, z.cells), i16)] * z.span,
        in_specs=[smem] * 4 + [hbm] * (1 + len(pieces)) + [vmem] * len(names),
        out_specs=[vmem] * z.span,
        scratch_shapes=[
            pltpu.VMEM((z.span, z.colors, z.rows, z.cells), bf16),
            pltpu.VMEM((wide, z.cells), f32),
            pltpu.VMEM((z.own, z.frame, z.cells), f32),
            pltpu.VMEM((wide, z.cells), f32),
            pltpu.VMEM((z.own * z.frame, z.cells), f32),
            pltpu.SemaphoreType.DMA((1 + len(pieces),)),
        ],
        compiler_params=pltpu.CompilerParams(vmem_limit_bytes=34 << 20),
        cost_estimate=pl.CostEstimate(flops=20_000_000_000, bytes_accessed=16_000_000, transcendentals=0),
        name="pair_solves",
    )(ids, count, slots, mine, here, *pieces, *[jnp.asarray(tables[n]) for n in names])


def plane_kernel(z, per_step, here, potential, plane, out):
    centre = here[...].reshape(per_step * z.rows, z.cells)
    tile, reach = 256, stencil_reach * z.box
    cols = []
    for j in range(0, z.cells, tile):
        lo, hi = max(0, j - reach) // tile * tile, -(-min(z.cells, j + tile + reach) // tile) * tile
        u = centre[:, lo:hi]
        cols.append(dot(u, plane[0, lo:hi, j : j + tile]) + dot(u, plane[1, lo:hi, j : j + tile]))
    flat = jnp.concatenate(cols, axis=1).reshape(per_step, z.rows, z.cells)
    out[...] = flat + potential[...][None] * here[...].astype(f32)


def plane_part(z, here, potential, plane):
    per_step = kin_colors * max(d for d in (1, 2, 3, 4) if z.colors // kin_colors % d == 0)
    block = pl.BlockSpec((per_step, z.rows, z.cells), lambda i: (i, 0, 0))
    vmem = pl.BlockSpec(memory_space=pltpu.VMEM)
    return pl.pallas_call(
        functools.partial(plane_kernel, z, per_step),
        grid=(z.colors // per_step,),
        out_shape=jax.ShapeDtypeStruct((z.colors, z.rows, z.cells), f32),
        in_specs=[block, vmem, vmem],
        out_specs=block,
        compiler_params=pltpu.CompilerParams(
            vmem_limit_bytes=16 << 20, dimension_semantics=("arbitrary",)
        ),
        cost_estimate=pl.CostEstimate(flops=6_000_000_000, bytes_accessed=12_000_000, transcendentals=0),
        name="plane",
    )(here, potential, plane)


def along_kernel(z, per_step, layout, ids, shift, here, flat, *rest):
    pieces, rest = rest[: len(layout)], rest[len(layout) :]
    along, out, near, lhs, sems = rest
    q, g = ids[0], ids[1]
    step = pl.program_id(0)

    @pl.when(step == 0)
    def _():
        copies = []
        for piece, ref in zip(layout, pieces):
            to = near.at[(piece.slab(q) > z.mid).astype(i32), piece.colors(g)]
            copies.append(pltpu.make_async_copy(ref, to, sems.at[len(copies)]))
        for c in copies:
            c.start()
        for c in copies:
            c.wait()

    rows, cells, kc = z.rows, z.cells, kin_colors
    lane = lax.broadcasted_iota(i32, (rows, 3 * kc * rows), 1)
    for s in range(per_step // kc):
        first = step * per_step + s * kc
        for i in range(kc):
            start = lax.rem(shift[first + i] - q * rows + z.grid, z.box)
            lhs[i * rows : (i + 1) * rows, :] = jnp.where(lane // rows % kc == i, along[start], 0.0)
        mid = here[s * kc : (s + 1) * kc].reshape(kc * rows, cells)
        before = near[0, pl.ds(first, kc)].reshape(kc * rows, cells)
        after = near[1, pl.ds(first, kc)].reshape(kc * rows, cells)
        stack = jnp.concatenate([before, mid, after], axis=0)
        head, low = split2(lhs[...])
        kin = (dot(head, stack) + dot(low, stack)).reshape(kc, rows, cells)
        out[s * kc : (s + 1) * kc] = flat[s * kc : (s + 1) * kc] + kin


def along_part(z, ids, shift, here, flat, layout, pieces, along):
    per_step = kin_colors * max(d for d in (1, 2, 3, 4) if z.colors // kin_colors % d == 0)
    smem = pl.BlockSpec(memory_space=pltpu.SMEM)
    hbm = pl.BlockSpec(memory_space=pl.ANY)
    block = pl.BlockSpec((per_step, z.rows, z.cells), lambda i: (i, 0, 0))
    vmem = pl.BlockSpec(memory_space=pltpu.VMEM)
    return pl.pallas_call(
        functools.partial(along_kernel, z, per_step, layout),
        grid=(z.colors // per_step,),
        out_shape=jax.ShapeDtypeStruct((z.colors, z.rows, z.cells), f32),
        in_specs=[smem, smem, block, block] + [hbm] * len(pieces) + [vmem],
        out_specs=block,
        scratch_shapes=[
            pltpu.VMEM((2, z.colors, z.rows, z.cells), bf16),
            pltpu.VMEM((kin_colors * z.rows, 3 * kin_colors * z.rows), f32),
            pltpu.SemaphoreType.DMA((len(pieces),)),
        ],
        compiler_params=pltpu.CompilerParams(
            vmem_limit_bytes=16 << 20, dimension_semantics=("arbitrary",)
        ),
        cost_estimate=pl.CostEstimate(flops=5_000_000_000, bytes_accessed=12_000_000, transcendentals=0),
        name="along",
    )(ids, shift, here, flat, *pieces, along)


def finish_kernel(z, spans, ids, dst, local, *rest):
    parts, (out, total, sem) = rest[:-3], rest[-3:]
    order = butterfly_order(z.groups)
    at = 0
    for backs in spans:
        for p in range(z.groups):
            ref, at = parts[at], at + 1
            for b, back in enumerate(backs):
                for m in range(z.own):
                    c = dst[((ids[1] ^ order[p]) * z.width + back) * z.own + m]
                    plane, lane = z.own + m * LANES // z.cells, m * LANES % z.cells
                    scale = scale_of(ref[b * z.planes + plane, :, lane : lane + LANES])
                    value = ref[b * z.planes + m].astype(f32)
                    wide = jnp.concatenate([scale] * (z.cells // LANES), axis=1)
                    total[c] = local[c] + value * wide
                    pltpu.make_async_copy(total.at[c], out.at[c], sem).start()
    pltpu.make_async_copy(total, out, sem).wait()


def finish(z, ids, dst, local, spans, parts):
    smem = pl.BlockSpec(memory_space=pltpu.SMEM)
    vmem = pl.BlockSpec(memory_space=pltpu.VMEM)
    return pl.pallas_call(
        functools.partial(finish_kernel, z, spans),
        out_shape=jax.ShapeDtypeStruct(local.shape, f32),
        in_specs=[smem, smem, vmem] + [vmem] * len(parts),
        out_specs=pl.BlockSpec(memory_space=pl.ANY),
        scratch_shapes=[pltpu.VMEM(local.shape, f32), pltpu.SemaphoreType.DMA],
        compiler_params=pltpu.CompilerParams(vmem_limit_bytes=16 << 20),
        name="finish",
    )(ids, dst, local, *parts)


def moved(x, source, slabs):
    return lax.ppermute(x, "orb", [(source(i) % slabs, i) for i in range(slabs)])


def from_slab(x, away, slabs):
    return moved(x, lambda i: i + away, slabs)


def swapped(x, bit, groups):
    return lax.ppermute(x, "group", [(i, i ^ bit) for i in range(groups)])


def shared(piece, groups):
    have, step = [piece], groups // 2
    while step:
        have += [swapped(x, step, groups) for x in have]
        step //= 2
    return have


def after(x, *others):
    return lax.optimization_barrier((x, *others))[0]


def fetch(z, orbitals, g, early_work, late_work):
    slabs, groups = z.slabs, z.groups
    layout, pieces = [], []

    if z.mid != 2 or slabs % 2 or groups < 2:
        done = *early_work(), late_work(orbitals)
        quarter = lax.dynamic_slice_in_dim(orbitals, g * z.part, z.part, 0)
        for k in range(z.span):
            if k != z.mid:
                pieces += shared(from_slab(quarter, k - z.mid, slabs), groups)
                layout += [Piece(k, k, flip, groups, z.part, 0, z.part) for flip in butterfly_order(groups)]
        return layout, pieces, done
    half, lo, hi = z.colors // 2, z.mid - 2, z.mid + 2
    mine = lax.dynamic_slice_in_dim(orbitals, lax.rem(g, 2) * half, half, 0)
    side = moved(mine, lambda i: i + 2 if i % 2 == 0 else i - 2, slabs)
    near = moved(mine, lambda i: i ^ 1, slabs)
    done = early_work()
    side = after(side, *done)
    far = moved(side, lambda i: i ^ 1, slabs)
    rest = moved(after(mine, side), lambda i: i - 2 if i % 2 == 0 else i + 2, slabs)
    flat = late_work(after(orbitals, side))
    far = after(far, flat)
    for x, even, odd in ((near, lo + 3, lo + 1), (side, hi, lo), (far, lo + 1, lo + 3), (rest, lo, hi)):
        for flip, y in enumerate((x, swapped(x, 1, groups))):
            layout.append(Piece(even, odd, flip, 2, half, 0, half))
            pieces.append(y)
    return layout, pieces, (*done, flat)


def body(orbitals, potential, box_shift, pair_partner, pair_member):
    slabs, groups = lax.axis_size("orb"), lax.axis_size("group")
    z = Sizes(orbitals, pair_partner, groups, slabs)
    q, g = lax.axis_index("orb"), lax.axis_index("group")
    ids = jnp.stack([q, g]).astype(i32)
    plane, along = [jnp.asarray(t) for t in stencil_tables(z)]
    layout, pieces, done = fetch(
        z,
        orbitals,
        g,
        lambda: plan(z, ids, box_shift, pair_partner, pair_member),
        lambda x: plane_part(z, x, potential, plane),
    )
    count, slots, home, dst, flat = done
    beside = [i for i, p in enumerate(layout) if {p.even, p.odd} <= {z.mid - 1, z.mid + 1}]
    local = along_part(
        z, ids, box_shift, orbitals, flat, [layout[i] for i in beside], [pieces[i] for i in beside], along
    )
    spread = pair_part(z, ids, count, slots, home, orbitals, layout, pieces)
    parts = [
        spread[k] if k == z.mid else from_slab(spread[k], z.mid - k, slabs) for k in range(z.span)
    ]
    parts[0] = parts[0] + parts[-1]
    spans = [(0, z.mid)] + [tuple(k for k in range(1, z.width) if k != z.mid)]
    shares = [
        y for ks in spans for y in shared(after(jnp.concatenate([parts[k] for k in ks], axis=0), local), groups)
    ]
    return finish(z, ids, dst, local, spans, shares)


def solution(mesh):
    placed = (P(None, "orb", None), P("orb", None), P(), P(), P())
    return jax.shard_map(
        body, mesh=mesh, in_specs=placed, out_specs=P(None, "orb", None), check_vma=False
    )
```

```python
import functools
import math
from typing import NamedTuple

import jax
import jax.numpy as jnp
import numpy as np
from jax import lax
from jax.experimental import pallas as pl
from jax.experimental.pallas import tpu as pltpu
from jax.sharding import PartitionSpec as P

lap_weights = (
    -5369.0 / 1800.0,
    12.0 / 7.0,
    -15.0 / 56.0,
    10.0 / 189.0,
    -1.0 / 112.0,
    2.0 / 1925.0,
    -1.0 / 16632.0,
)
stencil_reach = 6
mixing = 0.25
f32, bf16, i32, i16 = jnp.float32, jnp.bfloat16, jnp.int32, jnp.int16
kin_colors = 8
EMPTY = -(1 << 20)
LANES = 128
TOP = 32767.0
STEPS = 256.0


def split_np(values):
    head = np.asarray(values, np.float32).astype(bf16)
    rest = (values - head.astype(np.float64)).astype(np.float32).astype(bf16)
    return np.stack([head, rest])


def split2(x):
    head = x.astype(bf16)
    return head, (x - head.astype(f32)).astype(bf16)


def dot(a, b):
    return jnp.dot(a, b, preferred_element_type=f32)


def dot3(a, b):
    rows = a[0].shape[0]
    both = dot(jnp.concatenate(a, axis=0), b[0])
    return both[:rows] + (dot(a[0], b[1]) + both[rows:])


class Sizes:
    def __init__(self, orbitals, pair_partner, groups, slabs):
        self.colors, self.rows, self.cells = orbitals.shape
        self.groups, self.slabs = groups, slabs
        self.box = math.isqrt(self.cells)
        self.width = self.box // self.rows
        self.span = self.width + 1
        self.mid = self.width // 2
        self.home = self.colors // self.width
        self.blocks = pair_partner.shape[0] // slabs
        self.members = self.home // self.blocks
        self.slots = pair_partner.shape[1]
        self.grid = slabs * self.rows
        self.per = self.grid // self.box
        self.part = self.colors // groups
        self.own = self.home // groups
        self.frame = self.span * self.rows
        self.batch = max(1, 256 // self.frame)
        self.planes = self.own + -(-self.own * LANES // self.cells)
        self.staged = self.mid == 2 and slabs % 2 == 0 and groups >= 2
        self.cap = -(-self.blocks * self.slots // self.batch) * self.batch + self.batch


def butterfly_order(groups):
    order, step = [0], groups // 2
    while step:
        order += [o ^ step for o in order]
        step //= 2
    return order


def sine_matrix(box):
    count = np.arange(1, box + 1)
    return np.sqrt(2.0 / (box + 1)) * np.sin(np.pi * np.outer(count, count) / (box + 1))


def pair_tables(z):
    box, half = z.box, z.box // 2
    sine = sine_matrix(box)
    side = [np.arange(half), box - 1 - np.arange(half)]
    order = np.concatenate([(y[:, None] * box + x[None, :]).reshape(-1) for y in side for x in side])
    regroup = np.zeros((z.cells, z.cells))
    regroup[order, np.arange(z.cells)] = 1.0
    halves = [sine[0::2, :half], sine[1::2, :half]]
    forward = np.stack([np.kron(a, b).T for a in halves for b in halves])
    backward = np.stack([m.T for m in forward])
    single = 2.0 - 2.0 * np.cos(np.pi * np.arange(1, box + 1) / (box + 1))
    modes = [(single[py::2][:, None] + single[pz::2][None, :]).reshape(-1) for py in (0, 1) for pz in (0, 1)]
    scale = -mixing / (single[:, None] + np.concatenate(modes)[None, :])
    into = np.zeros((z.rows, box, z.batch * z.frame))
    back = np.zeros((z.rows, z.frame, z.batch * box))
    for sub in range(z.rows):
        for i in range(z.batch):
            into[sub, :, i * z.frame + sub : i * z.frame + sub + box] = sine
            back[sub, sub : sub + box, i * box : (i + 1) * box] = sine.T
    return dict(
        regroup=regroup.astype(bf16),
        ungroup=regroup.T.astype(bf16),
        forward=split_np(forward),
        backward=split_np(backward),
        scale=scale.astype(np.float32),
        into=into.astype(np.float32),
        back=back.astype(np.float32),
    )


def stencil_tables(z):
    box, rows = z.box, z.rows
    band = np.zeros((box, box))
    for off in range(1, stencil_reach + 1):
        band += lap_weights[off] * (np.eye(box, k=off) + np.eye(box, k=-off))
    eye = np.eye(box)
    plane = -0.5 * (3.0 * lap_weights[0] * np.eye(z.cells) + np.kron(band, eye) + np.kron(eye, band))
    along = np.zeros((box, rows, 3 * kin_colors * rows))
    for start in range(box):
        for x in range(rows):
            for y in range(-rows, 2 * rows):
                off = abs(y - x)
                if off and off <= stencil_reach and (x - start) // box == (y - start) // box:
                    for i in range(kin_colors):
                        at = ((y + rows) // rows) * kin_colors * rows + i * rows + y % rows
                        along[start, x, at] = -0.5 * lap_weights[off]
    return split_np(plane), along.astype(np.float32)


def plan_kernel(z, ids, shift, partner, member, count_ref, slot_ref, mine_ref, dst_ref, order, filled):
    q, g = ids[0], ids[1]
    o = lax.rem(q + z.slabs - z.mid, z.slabs)
    for c in range(z.width):
        filled[c] = 0

    def color_step(c, _):
        cls = shift[c] // z.rows
        n = filled[cls]
        filled[cls] = n + 1
        order[cls, n] = c
        back = lax.rem(q - cls + z.slabs * z.width, z.width)
        dst_ref[(lax.rem(n, z.groups) * z.width + back) * z.own + n // z.groups] = c
        return 0

    lax.fori_loop(0, z.colors, color_step, 0)
    home_class = lax.rem(o, z.width)
    for m in range(z.own):
        c = order[home_class, m * z.groups + g]
        mine_ref[0, m] = c
        mine_ref[1, m] = lax.rem(shift[c], z.rows)
    reach_slots = z.slots // (2 * z.width - 1)
    sign = jnp.where(lax.rem(q, 2) == 0, 1, -1)
    counts = (jnp.int32(0), jnp.int32(0))
    for t in range(z.blocks):

        def slot_step(p, counts, t=t):
            j = partner[o * z.blocks + t, p]
            n = t * z.members + member[o * z.blocks + t, p]
            live = jnp.logical_and(j >= 0, lax.rem(n, z.groups) == g)
            j = jnp.maximum(j, 0)
            cj = j // z.per
            sub = lax.rem(shift[order[home_class, n]], z.rows)
            there = (j - cj * z.per) * z.box + shift[cj]
            d = there - (o * z.rows + sub) + z.grid // 2
            d = lax.rem(d + z.grid, z.grid) - z.grid // 2
            reach = (p // reach_slots - (z.width - 1)) * sign
            first = jnp.logical_and(reach >= z.mid, z.staged).astype(i32)
            at = jnp.where(first == 1, counts[0], counts[1])
            slot_ref[first, 0, at] = n // z.groups
            slot_ref[first, 1, at] = cj
            slot_ref[first, 2, at] = sub + d
            slot_ref[first, 3, at] = sub
            one = live.astype(i32)
            return counts[0] + one * first, counts[1] + one * (1 - first)

        counts = lax.fori_loop(0, z.slots, slot_step, counts)
    for first in (0, 1):
        total = counts[1 - first]
        count_ref[first] = total
        for i in range(z.batch):
            slot_ref[first, 0, total + i] = 0
            slot_ref[first, 1, total + i] = 0
            slot_ref[first, 2, total + i] = EMPTY
            slot_ref[first, 3, total + i] = 0


def plan(z, ids, shift, partner, member):
    smem = pl.BlockSpec(memory_space=pltpu.SMEM)
    return pl.pallas_call(
        functools.partial(plan_kernel, z),
        out_shape=(
            jax.ShapeDtypeStruct((2,), i32),
            jax.ShapeDtypeStruct((2, 4, z.cap), i32),
            jax.ShapeDtypeStruct((2, z.own), i32),
            jax.ShapeDtypeStruct((z.colors,), i32),
        ),
        in_specs=[smem] * 4,
        out_specs=(smem,) * 4,
        scratch_shapes=[pltpu.SMEM((z.width, z.colors), i32), pltpu.SMEM((z.width,), i32)],
        cost_estimate=pl.CostEstimate(flops=10_000_000_000, bytes_accessed=100_000, transcendentals=0),
        name="plan",
    )(ids, shift, partner, member)


class Piece(NamedTuple):
    even: int
    odd: int
    flip: int
    parts: int
    unit: int
    add: int
    size: int

    def slab(self, q):
        return jnp.where(lax.rem(q, 2) == 0, self.even, self.odd)

    def colors(self, g):
        return pl.ds(lax.rem(g ^ self.flip, self.parts) * self.unit + self.add, self.size)


def scale_of(code):
    return jnp.exp2(code.astype(f32) * (1.0 / STEPS)) * (1.0 / TOP)


def coded(x):
    groups = [x[:, i : i + LANES] for i in range(0, x.shape[1], LANES)]
    top = functools.reduce(jnp.maximum, [jnp.abs(v) for v in groups])
    code = jnp.ceil(jnp.log2(jnp.clip(top, 2.0**-100, 2.0**100)) * STEPS) + 1.0
    factor = 1.0 / scale_of(code)
    whole = [jnp.clip(jnp.round(v * factor), -TOP, TOP).astype(i32) for v in groups]
    return jnp.concatenate(whole, axis=1), jnp.where(top > 0, code, 0.0).astype(i32)


def pair_kernel(z, first, layout, ids, count, slots, mine, here, *rest):
    pieces, rest = rest[: len(layout)], rest[len(layout) :]
    if not first:
        sums, rest = rest[0], rest[1:]
    (regroup, forward, backward, scale, into, back), rest = rest[:6], rest[6:]
    if first:
        acc, window, raw, own, held, sems = rest
    else:
        ungroup, outs, (window, raw, own, held, acc, sems) = rest[0], rest[1 : z.span + 1], rest[z.span + 1 :]
    which = 1 if first else 0
    q, g = ids[0], ids[1]
    copies = [pltpu.make_async_copy(here, window.at[z.mid], sems.at[0])]
    for piece, ref in zip(layout, pieces):
        to = window.at[piece.slab(q), piece.colors(g)]
        copies.append(pltpu.make_async_copy(ref, to, sems.at[len(copies)]))
    for c in copies:
        c.start()
    acc[...] = jnp.zeros(acc.shape, f32) if first else sums[...]
    for c in copies:
        c.wait()
    frame, box, batch, quad = z.frame, z.box, z.batch, z.cells // 4
    rows = lax.broadcasted_iota(i32, (z.rows, z.cells), 0)

    def regrouped():
        return dot(raw[...].astype(bf16), regroup[...])

    for start in range(0, z.own, batch):
        todo = min(batch, z.own - start)
        for i in range(batch):
            for k in range(z.span):
                at = i * frame + k * z.rows
                if i < todo:
                    value = window[k, mine[0, start + i]].astype(f32)
                    if first and k != z.mid:
                        here_now = (k > z.mid) == (lax.rem(q, 2) == 0)
                        value = jnp.where(here_now, value, 0.0)
                    raw[at : at + z.rows, :] = value
                else:
                    raw[at : at + z.rows, :] = jnp.zeros((z.rows, z.cells), f32)
        done = regrouped()
        for i in range(todo):
            own[start + i] = done[i * frame : (i + 1) * frame]

    lane_in = lax.broadcasted_iota(i32, (box, batch * frame), 1)
    lane_back = lax.broadcasted_iota(i32, (frame, batch * box), 1)

    def step(b, _):
        base = b * batch
        for i in range(batch):
            color, start = slots[which, 1, base + i], slots[which, 2, base + i]
            for k in range(z.span):
                at = i * frame + k * z.rows
                r = rows + (k * z.rows - start)
                inside = (r >= 0) & (r < box)
                raw[at : at + z.rows, :] = jnp.where(inside, window[k, color].astype(f32), 0.0)
        held[...] = regrouped()
        lhs_in, lhs_back, density = [], [], []
        for i in range(batch):
            m, sub = slots[which, 0, base + i], slots[which, 3, base + i]
            lo = i * frame
            lhs_in.append(jnp.where((lane_in >= lo) & (lane_in < lo + frame), into[sub], 0.0))
            lo = i * box
            lhs_back.append(jnp.where((lane_back >= lo) & (lane_back < lo + box), back[sub], 0.0))
            density.append(own[m] * held[i * frame : (i + 1) * frame])
        x = dot3(split2(jnp.concatenate(lhs_in, 0)), split2(jnp.concatenate(density, 0)))
        q = [x[:, i * quad : (i + 1) * quad] for i in range(4)]
        a, b_, c, d = q[0] + q[2], q[0] - q[2], q[1] + q[3], q[1] - q[3]
        folded = (a + c, a - c, b_ + d, b_ - d)
        solved = []
        for i in range(4):
            y = dot3(split2(folded[i]), (forward[0, i], forward[1, i]))
            factor = scale[:, i * quad : (i + 1) * quad]
            y = (y.reshape(batch, box, quad) * factor[None]).reshape(batch * box, quad)
            solved.append(dot3(split2(y), (backward[0, i], backward[1, i])))
        ee, eo, oe, oo = solved
        a, b_, c, d = ee + oe, ee - oe, eo + oo, eo - oo
        field = jnp.concatenate([a + c, a - c, b_ + d, b_ - d], axis=1)
        v = dot3(split2(jnp.concatenate(lhs_back, 0)), split2(field))
        for i in range(batch):
            at = pl.ds(slots[which, 0, base + i] * frame, frame)
            lo = i * frame
            acc[at, :] = acc[at, :] + v[lo : lo + frame] * held[lo : lo + frame]
        return 0

    lax.fori_loop(0, (count[which] + batch - 1) // batch, step, 0)
    if first:
        return
    head, low = split2(acc[...])
    res = dot(head, ungroup[...]) + dot(low, ungroup[...])
    values, codes = coded(res)
    for m in range(z.own):
        for k in range(z.span):
            at = m * frame + k * z.rows
            outs[k][m] = values[at : at + z.rows].astype(i16)
            plane, lane = z.own + m * LANES // z.cells, m * LANES % z.cells
            outs[k][plane, :, lane : lane + LANES] = codes[at : at + z.rows].astype(i16)


def pair_part(z, ids, count, slots, mine, here, layout, pieces, sums=None):
    first = sums is None
    tables = pair_tables(z)
    smem = pl.BlockSpec(memory_space=pltpu.SMEM)
    vmem = pl.BlockSpec(memory_space=pltpu.VMEM)
    hbm = pl.BlockSpec(memory_space=pl.ANY)
    names = ("regroup", "forward", "backward", "scale", "into", "back") + (() if first else ("ungroup",))
    wide, total = z.batch * z.frame, (z.own * z.frame, z.cells)
    if first:
        given, shapes = [], jax.ShapeDtypeStruct(total, f32)
    else:
        given, shapes = [sums], [jax.ShapeDtypeStruct((z.planes, z.rows, z.cells), i16)] * z.span
    return pl.pallas_call(
        functools.partial(pair_kernel, z, first, layout),
        out_shape=shapes,
        in_specs=[smem] * 4 + [hbm] * (1 + len(pieces)) + [vmem] * (len(given) + len(names)),
        out_specs=vmem if first else [vmem] * z.span,
        scratch_shapes=[
            pltpu.VMEM((z.span, z.colors, z.rows, z.cells), bf16),
            pltpu.VMEM((wide, z.cells), f32),
            pltpu.VMEM((z.own, z.frame, z.cells), f32),
            pltpu.VMEM((wide, z.cells), f32),
            *([] if first else [pltpu.VMEM(total, f32)]),
            pltpu.SemaphoreType.DMA((1 + len(pieces),)),
        ],
        compiler_params=pltpu.CompilerParams(vmem_limit_bytes=34 << 20),
        cost_estimate=pl.CostEstimate(
            flops=8_000_000_000 if first else 20_000_000_000, bytes_accessed=16_000_000, transcendentals=0
        ),
        name="first_pairs" if first else "pair_solves",
    )(ids, count, slots, mine, here, *pieces, *given, *[jnp.asarray(tables[n]) for n in names])


def plane_kernel(z, per_step, here, potential, plane, out):
    centre = here[...].reshape(per_step * z.rows, z.cells)
    tile, reach = 256, stencil_reach * z.box
    cols = []
    for j in range(0, z.cells, tile):
        lo, hi = max(0, j - reach) // tile * tile, -(-min(z.cells, j + tile + reach) // tile) * tile
        u = centre[:, lo:hi]
        cols.append(dot(u, plane[0, lo:hi, j : j + tile]) + dot(u, plane[1, lo:hi, j : j + tile]))
    flat = jnp.concatenate(cols, axis=1).reshape(per_step, z.rows, z.cells)
    out[...] = flat + potential[...][None] * here[...].astype(f32)


def plane_part(z, here, potential, plane):
    per_step = kin_colors * max(d for d in (1, 2, 3, 4) if z.colors // kin_colors % d == 0)
    block = pl.BlockSpec((per_step, z.rows, z.cells), lambda i: (i, 0, 0))
    vmem = pl.BlockSpec(memory_space=pltpu.VMEM)
    return pl.pallas_call(
        functools.partial(plane_kernel, z, per_step),
        grid=(z.colors // per_step,),
        out_shape=jax.ShapeDtypeStruct((z.colors, z.rows, z.cells), f32),
        in_specs=[block, vmem, vmem],
        out_specs=block,
        compiler_params=pltpu.CompilerParams(
            vmem_limit_bytes=16 << 20, dimension_semantics=("arbitrary",)
        ),
        cost_estimate=pl.CostEstimate(flops=6_000_000_000, bytes_accessed=12_000_000, transcendentals=0),
        name="plane",
    )(here, potential, plane)


def along_kernel(z, per_step, layout, ids, shift, here, flat, *rest):
    pieces, rest = rest[: len(layout)], rest[len(layout) :]
    along, out, near, lhs, sems = rest
    q, g = ids[0], ids[1]
    step = pl.program_id(0)

    @pl.when(step == 0)
    def _():
        copies = []
        for piece, ref in zip(layout, pieces):
            to = near.at[(piece.slab(q) > z.mid).astype(i32), piece.colors(g)]
            copies.append(pltpu.make_async_copy(ref, to, sems.at[len(copies)]))
        for c in copies:
            c.start()
        for c in copies:
            c.wait()

    rows, cells, kc = z.rows, z.cells, kin_colors
    lane = lax.broadcasted_iota(i32, (rows, 3 * kc * rows), 1)
    for s in range(per_step // kc):
        first = step * per_step + s * kc
        for i in range(kc):
            start = lax.rem(shift[first + i] - q * rows + z.grid, z.box)
            lhs[i * rows : (i + 1) * rows, :] = jnp.where(lane // rows % kc == i, along[start], 0.0)
        mid = here[s * kc : (s + 1) * kc].reshape(kc * rows, cells)
        before = near[0, pl.ds(first, kc)].reshape(kc * rows, cells)
        after = near[1, pl.ds(first, kc)].reshape(kc * rows, cells)
        stack = jnp.concatenate([before, mid, after], axis=0)
        head, low = split2(lhs[...])
        kin = (dot(head, stack) + dot(low, stack)).reshape(kc, rows, cells)
        out[s * kc : (s + 1) * kc] = flat[s * kc : (s + 1) * kc] + kin


def along_part(z, ids, shift, here, flat, layout, pieces, along):
    per_step = kin_colors * max(d for d in (1, 2, 3, 4) if z.colors // kin_colors % d == 0)
    smem = pl.BlockSpec(memory_space=pltpu.SMEM)
    hbm = pl.BlockSpec(memory_space=pl.ANY)
    block = pl.BlockSpec((per_step, z.rows, z.cells), lambda i: (i, 0, 0))
    vmem = pl.BlockSpec(memory_space=pltpu.VMEM)
    return pl.pallas_call(
        functools.partial(along_kernel, z, per_step, layout),
        grid=(z.colors // per_step,),
        out_shape=jax.ShapeDtypeStruct((z.colors, z.rows, z.cells), f32),
        in_specs=[smem, smem, block, block] + [hbm] * len(pieces) + [vmem],
        out_specs=block,
        scratch_shapes=[
            pltpu.VMEM((2, z.colors, z.rows, z.cells), bf16),
            pltpu.VMEM((kin_colors * z.rows, 3 * kin_colors * z.rows), f32),
            pltpu.SemaphoreType.DMA((len(pieces),)),
        ],
        compiler_params=pltpu.CompilerParams(
            vmem_limit_bytes=16 << 20, dimension_semantics=("arbitrary",)
        ),
        cost_estimate=pl.CostEstimate(flops=5_000_000_000, bytes_accessed=12_000_000, transcendentals=0),
        name="along",
    )(ids, shift, here, flat, *pieces, along)


def finish_kernel(z, spans, ids, dst, local, *rest):
    parts, (out, total, sem) = rest[:-3], rest[-3:]
    order = butterfly_order(z.groups)
    at = 0
    for backs in spans:
        for p in range(z.groups):
            ref, at = parts[at], at + 1
            for b, back in enumerate(backs):
                for m in range(z.own):
                    c = dst[((ids[1] ^ order[p]) * z.width + back) * z.own + m]
                    plane, lane = z.own + m * LANES // z.cells, m * LANES % z.cells
                    scale = scale_of(ref[b * z.planes + plane, :, lane : lane + LANES])
                    value = ref[b * z.planes + m].astype(f32)
                    wide = jnp.concatenate([scale] * (z.cells // LANES), axis=1)
                    total[c] = local[c] + value * wide
                    pltpu.make_async_copy(total.at[c], out.at[c], sem).start()
    pltpu.make_async_copy(total, out, sem).wait()


def finish(z, ids, dst, local, spans, parts):
    smem = pl.BlockSpec(memory_space=pltpu.SMEM)
    vmem = pl.BlockSpec(memory_space=pltpu.VMEM)
    return pl.pallas_call(
        functools.partial(finish_kernel, z, spans),
        out_shape=jax.ShapeDtypeStruct(local.shape, f32),
        in_specs=[smem, smem, vmem] + [vmem] * len(parts),
        out_specs=pl.BlockSpec(memory_space=pl.ANY),
        scratch_shapes=[pltpu.VMEM(local.shape, f32), pltpu.SemaphoreType.DMA],
        compiler_params=pltpu.CompilerParams(vmem_limit_bytes=16 << 20),
        name="finish",
    )(ids, dst, local, *parts)


def moved(x, source, slabs):
    return lax.ppermute(x, "orb", [(source(i) % slabs, i) for i in range(slabs)])


def from_slab(x, away, slabs):
    return moved(x, lambda i: i + away, slabs)


def swapped(x, bit, groups):
    return lax.ppermute(x, "group", [(i, i ^ bit) for i in range(groups)])


def shared(piece, groups, *others):
    have, step = [piece], groups // 2
    while step:
        if step == 1 and others:
            have = [after(x, *others) for x in have]
        have += [swapped(x, step, groups) for x in have]
        step //= 2
    return have


def after(x, *others):
    return lax.optimization_barrier((x, *others))[0]


def fetch(z, orbitals, g, early_work, late_work, first_pairs):
    slabs, groups = z.slabs, z.groups
    layout, pieces = [], []

    if not z.staged:
        done = early_work()
        flat = late_work(orbitals)
        sums = first_pairs(done, [], [])
        quarter = lax.dynamic_slice_in_dim(orbitals, g * z.part, z.part, 0)
        for k in range(z.span):
            if k != z.mid:
                pieces += shared(from_slab(quarter, k - z.mid, slabs), groups)
                layout += [Piece(k, k, flip, groups, z.part, 0, z.part) for flip in butterfly_order(groups)]
        return layout, pieces, (*done, flat, sums)
    half, lo, hi = z.colors // 2, z.mid - 2, z.mid + 2
    mine = lax.dynamic_slice_in_dim(orbitals, lax.rem(g, 2) * half, half, 0)
    side = moved(mine, lambda i: i + 2 if i % 2 == 0 else i - 2, slabs)
    near = moved(mine, lambda i: i ^ 1, slabs)
    done = early_work()
    side = after(side, *done)
    far = moved(side, lambda i: i ^ 1, slabs)
    rest = moved(after(mine, side), lambda i: i - 2 if i % 2 == 0 else i + 2, slabs)
    flat = late_work(after(orbitals, side))

    def keep(x, even, odd):
        for flip, y in enumerate((x, swapped(x, 1, groups))):
            layout.append(Piece(even, odd, flip, 2, half, 0, half))
            pieces.append(y)

    keep(near, lo + 3, lo + 1)
    keep(side, hi, lo)
    sums = first_pairs(done, list(layout), list(pieces))
    keep(after(far, flat), lo + 1, lo + 3)
    keep(after(rest, sums), lo, hi)
    return layout, pieces, (*done, flat, sums)


def body(orbitals, potential, box_shift, pair_partner, pair_member):
    slabs, groups = lax.axis_size("orb"), lax.axis_size("group")
    z = Sizes(orbitals, pair_partner, groups, slabs)
    q, g = lax.axis_index("orb"), lax.axis_index("group")
    ids = jnp.stack([q, g]).astype(i32)
    plane, along = [jnp.asarray(t) for t in stencil_tables(z)]
    layout, pieces, done = fetch(
        z,
        orbitals,
        g,
        lambda: plan(z, ids, box_shift, pair_partner, pair_member),
        lambda x: plane_part(z, x, potential, plane),
        lambda planned, layout, pieces: pair_part(z, ids, *planned[:3], orbitals, layout, pieces),
    )
    count, slots, home, dst, flat, sums = done
    spread = pair_part(z, ids, count, slots, home, orbitals, layout, pieces, sums)
    parts = [
        spread[k] if k == z.mid else from_slab(spread[k], z.mid - k, slabs) for k in range(z.span)
    ]
    parts[0] = parts[0] + parts[-1]
    spans = [(z.mid,), tuple(range(z.mid + 1, z.width)), tuple(range(z.mid))]
    middle = shared(parts[z.mid], groups)
    near = jnp.concatenate([parts[k] for k in spans[1]], axis=0)
    beside = [i for i, p in enumerate(layout) if {p.even, p.odd} <= {z.mid - 1, z.mid + 1}]
    local = along_part(
        z,
        ids,
        box_shift,
        orbitals,
        after(flat, near),
        [layout[i] for i in beside],
        [pieces[i] for i in beside],
        along,
    )
    far = jnp.concatenate([parts[k] for k in spans[2]], axis=0)
    near, far = shared(near, groups), shared(far, groups, local)
    return finish(z, ids, dst, local, spans, middle + near + far)


def solution(mesh):
    placed = (P(None, "orb", None), P("orb", None), P(), P(), P())
    return jax.shard_map(
        body, mesh=mesh, in_specs=placed, out_specs=P(None, "orb", None), check_vma=False
    )
```

```python
import functools
import math
from typing import NamedTuple

import jax
import jax.numpy as jnp
import numpy as np
from jax import lax
from jax.experimental import pallas as pl
from jax.experimental.pallas import tpu as pltpu
from jax.sharding import PartitionSpec as P

lap_weights = (
    -5369.0 / 1800.0,
    12.0 / 7.0,
    -15.0 / 56.0,
    10.0 / 189.0,
    -1.0 / 112.0,
    2.0 / 1925.0,
    -1.0 / 16632.0,
)
stencil_reach = 6
mixing = 0.25
f32, bf16, i32, i16 = jnp.float32, jnp.bfloat16, jnp.int32, jnp.int16
kin_colors = 8
EMPTY = -(1 << 20)
LANES = 128
TOP = 32767.0
STEPS = 256.0


def split_np(values):
    head = np.asarray(values, np.float32).astype(bf16)
    rest = (values - head.astype(np.float64)).astype(np.float32).astype(bf16)
    return np.stack([head, rest])


def split2(x):
    head = x.astype(bf16)
    return head, (x - head.astype(f32)).astype(bf16)


def dot(a, b):
    return jnp.dot(a, b, preferred_element_type=f32)


def dot3(a, b):
    rows = a[0].shape[0]
    both = dot(jnp.concatenate(a, axis=0), b[0])
    return both[:rows] + (dot(a[0], b[1]) + both[rows:])


class Sizes:
    def __init__(self, orbitals, pair_partner, groups, slabs):
        self.colors, self.rows, self.cells = orbitals.shape
        self.groups, self.slabs = groups, slabs
        self.box = math.isqrt(self.cells)
        self.width = self.box // self.rows
        self.span = self.width + 1
        self.mid = self.width // 2
        self.home = self.colors // self.width
        self.blocks = pair_partner.shape[0] // slabs
        self.members = self.home // self.blocks
        self.slots = pair_partner.shape[1]
        self.grid = slabs * self.rows
        self.per = self.grid // self.box
        self.part = self.colors // groups
        self.own = self.home // groups
        self.frame = self.span * self.rows
        self.batch = max(1, 256 // self.frame)
        self.planes = self.own + -(-self.own * LANES // self.cells)
        self.staged = self.mid == 2 and slabs % 2 == 0 and groups >= 2
        self.cap = -(-self.blocks * self.slots // self.batch) * self.batch + self.batch


def butterfly_order(groups):
    order, step = [0], groups // 2
    while step:
        order += [o ^ step for o in order]
        step //= 2
    return order


def sine_matrix(box):
    count = np.arange(1, box + 1)
    return np.sqrt(2.0 / (box + 1)) * np.sin(np.pi * np.outer(count, count) / (box + 1))


def pair_tables(z):
    box, half = z.box, z.box // 2
    sine = sine_matrix(box)
    side = [np.arange(half), box - 1 - np.arange(half)]
    order = np.concatenate([(y[:, None] * box + x[None, :]).reshape(-1) for y in side for x in side])
    regroup = np.zeros((z.cells, z.cells))
    regroup[order, np.arange(z.cells)] = 1.0
    halves = [sine[0::2, :half], sine[1::2, :half]]
    forward = np.stack([np.kron(a, b).T for a in halves for b in halves])
    backward = np.stack([m.T for m in forward])
    single = 2.0 - 2.0 * np.cos(np.pi * np.arange(1, box + 1) / (box + 1))
    modes = [(single[py::2][:, None] + single[pz::2][None, :]).reshape(-1) for py in (0, 1) for pz in (0, 1)]
    scale = -mixing / (single[:, None] + np.concatenate(modes)[None, :])
    into = np.zeros((z.rows, box, z.batch * z.frame))
    back = np.zeros((z.rows, z.frame, z.batch * box))
    for sub in range(z.rows):
        for i in range(z.batch):
            into[sub, :, i * z.frame + sub : i * z.frame + sub + box] = sine
            back[sub, sub : sub + box, i * box : (i + 1) * box] = sine.T
    return dict(
        regroup=regroup.astype(bf16),
        ungroup=regroup.T.astype(bf16),
        forward=split_np(forward),
        backward=split_np(backward),
        scale=scale.astype(np.float32),
        into=into.astype(np.float32),
        back=back.astype(np.float32),
    )


def stencil_tables(z):
    box, rows = z.box, z.rows
    band = np.zeros((box, box))
    for off in range(1, stencil_reach + 1):
        band += lap_weights[off] * (np.eye(box, k=off) + np.eye(box, k=-off))
    eye = np.eye(box)
    plane = -0.5 * (3.0 * lap_weights[0] * np.eye(z.cells) + np.kron(band, eye) + np.kron(eye, band))
    along = np.zeros((box, rows, 3 * kin_colors * rows))
    for start in range(box):
        for x in range(rows):
            for y in range(-rows, 2 * rows):
                off = abs(y - x)
                if off and off <= stencil_reach and (x - start) // box == (y - start) // box:
                    for i in range(kin_colors):
                        at = ((y + rows) // rows) * kin_colors * rows + i * rows + y % rows
                        along[start, x, at] = -0.5 * lap_weights[off]
    return split_np(plane), along.astype(np.float32)


def plan_kernel(z, ids, shift, partner, member, count_ref, slot_ref, mine_ref, dst_ref, order, filled):
    q, g = ids[0], ids[1]
    o = lax.rem(q + z.slabs - z.mid, z.slabs)
    for c in range(z.width):
        filled[c] = 0

    def color_step(c, _):
        cls = shift[c] // z.rows
        n = filled[cls]
        filled[cls] = n + 1
        order[cls, n] = c
        back = lax.rem(q - cls + z.slabs * z.width, z.width)
        dst_ref[(lax.rem(n, z.groups) * z.width + back) * z.own + n // z.groups] = c
        return 0

    lax.fori_loop(0, z.colors, color_step, 0)
    home_class = lax.rem(o, z.width)
    for m in range(z.own):
        c = order[home_class, m * z.groups + g]
        mine_ref[0, m] = c
        mine_ref[1, m] = lax.rem(shift[c], z.rows)
    reach_slots = z.slots // (2 * z.width - 1)
    sign = jnp.where(lax.rem(q, 2) == 0, 1, -1)
    counts = (jnp.int32(0), jnp.int32(0))
    for t in range(z.blocks):

        def slot_step(p, counts, t=t):
            j = partner[o * z.blocks + t, p]
            n = t * z.members + member[o * z.blocks + t, p]
            live = jnp.logical_and(j >= 0, lax.rem(n, z.groups) == g)
            j = jnp.maximum(j, 0)
            cj = j // z.per
            sub = lax.rem(shift[order[home_class, n]], z.rows)
            there = (j - cj * z.per) * z.box + shift[cj]
            d = there - (o * z.rows + sub) + z.grid // 2
            d = lax.rem(d + z.grid, z.grid) - z.grid // 2
            reach = (p // reach_slots - (z.width - 1)) * sign
            first = jnp.logical_and(reach >= z.mid, z.staged).astype(i32)
            at = jnp.where(first == 1, counts[0], counts[1])
            slot_ref[first, 0, at] = n // z.groups
            slot_ref[first, 1, at] = cj
            slot_ref[first, 2, at] = sub + d
            slot_ref[first, 3, at] = sub
            one = live.astype(i32)
            return counts[0] + one * first, counts[1] + one * (1 - first)

        counts = lax.fori_loop(0, z.slots, slot_step, counts)
    for first in (0, 1):
        total = counts[1 - first]
        count_ref[first] = total
        for i in range(z.batch):
            slot_ref[first, 0, total + i] = 0
            slot_ref[first, 1, total + i] = 0
            slot_ref[first, 2, total + i] = EMPTY
            slot_ref[first, 3, total + i] = 0


def plan(z, ids, shift, partner, member):
    smem = pl.BlockSpec(memory_space=pltpu.SMEM)
    return pl.pallas_call(
        functools.partial(plan_kernel, z),
        out_shape=(
            jax.ShapeDtypeStruct((2,), i32),
            jax.ShapeDtypeStruct((2, 4, z.cap), i32),
            jax.ShapeDtypeStruct((2, z.own), i32),
            jax.ShapeDtypeStruct((z.colors,), i32),
        ),
        in_specs=[smem] * 4,
        out_specs=(smem,) * 4,
        scratch_shapes=[pltpu.SMEM((z.width, z.colors), i32), pltpu.SMEM((z.width,), i32)],
        cost_estimate=pl.CostEstimate(flops=10_000_000_000, bytes_accessed=100_000, transcendentals=0),
        name="plan",
    )(ids, shift, partner, member)


class Piece(NamedTuple):
    even: int
    odd: int
    flip: int
    parts: int
    unit: int
    add: int
    size: int

    def slab(self, q):
        return jnp.where(lax.rem(q, 2) == 0, self.even, self.odd)

    def colors(self, g):
        return pl.ds(lax.rem(g ^ self.flip, self.parts) * self.unit + self.add, self.size)


def scale_of(code):
    return jnp.exp2(code.astype(f32) * (1.0 / STEPS)) * (1.0 / TOP)


def coded(x):
    groups = [x[:, i : i + LANES] for i in range(0, x.shape[1], LANES)]
    top = functools.reduce(jnp.maximum, [jnp.abs(v) for v in groups])
    code = jnp.ceil(jnp.log2(jnp.clip(top, 2.0**-100, 2.0**100)) * STEPS) + 1.0
    factor = 1.0 / scale_of(code)
    whole = [jnp.clip(jnp.round(v * factor), -TOP, TOP).astype(i32) for v in groups]
    return jnp.concatenate(whole, axis=1), jnp.where(top > 0, code, 0.0).astype(i32)


def pair_kernel(z, first, layout, ids, count, slots, mine, here, *rest):
    pieces, rest = rest[: len(layout)], rest[len(layout) :]
    if not first:
        sums, rest = rest[0], rest[1:]
    (regroup, forward, backward, scale, into, back), rest = rest[:6], rest[6:]
    if first:
        acc, window, raw, own, held, sems = rest
    else:
        ungroup, outs, (window, raw, own, held, acc, sems) = rest[0], rest[1 : z.span + 1], rest[z.span + 1 :]
    which = 1 if first else 0
    q, g = ids[0], ids[1]
    copies = [pltpu.make_async_copy(here, window.at[z.mid], sems.at[0])]
    for piece, ref in zip(layout, pieces):
        to = window.at[piece.slab(q), piece.colors(g)]
        copies.append(pltpu.make_async_copy(ref, to, sems.at[len(copies)]))
    for c in copies:
        c.start()
    acc[...] = jnp.zeros(acc.shape, f32) if first else sums[...]
    for c in copies:
        c.wait()
    frame, box, batch, quad = z.frame, z.box, z.batch, z.cells // 4
    rows = lax.broadcasted_iota(i32, (z.rows, z.cells), 0)

    def regrouped():
        return dot(raw[...].astype(bf16), regroup[...])

    for start in range(0, z.own, batch):
        todo = min(batch, z.own - start)
        for i in range(batch):
            for k in range(z.span):
                at = i * frame + k * z.rows
                if i < todo:
                    value = window[k, mine[0, start + i]].astype(f32)
                    if first and k != z.mid:
                        here_now = (k > z.mid) == (lax.rem(q, 2) == 0)
                        value = jnp.where(here_now, value, 0.0)
                    raw[at : at + z.rows, :] = value
                else:
                    raw[at : at + z.rows, :] = jnp.zeros((z.rows, z.cells), f32)
        done = regrouped()
        for i in range(todo):
            own[start + i] = done[i * frame : (i + 1) * frame]

    lane_in = lax.broadcasted_iota(i32, (box, batch * frame), 1)
    lane_back = lax.broadcasted_iota(i32, (frame, batch * box), 1)

    def step(b, _):
        base = b * batch
        for i in range(batch):
            color, start = slots[which, 1, base + i], slots[which, 2, base + i]
            for k in range(z.span):
                at = i * frame + k * z.rows
                r = rows + (k * z.rows - start)
                inside = (r >= 0) & (r < box)
                raw[at : at + z.rows, :] = jnp.where(inside, window[k, color].astype(f32), 0.0)
        held[...] = regrouped()
        lhs_in, lhs_back, density = [], [], []
        for i in range(batch):
            m, sub = slots[which, 0, base + i], slots[which, 3, base + i]
            lo = i * frame
            lhs_in.append(jnp.where((lane_in >= lo) & (lane_in < lo + frame), into[sub], 0.0))
            lo = i * box
            lhs_back.append(jnp.where((lane_back >= lo) & (lane_back < lo + box), back[sub], 0.0))
            density.append(own[m] * held[i * frame : (i + 1) * frame])
        x = dot3(split2(jnp.concatenate(lhs_in, 0)), split2(jnp.concatenate(density, 0)))
        q = [x[:, i * quad : (i + 1) * quad] for i in range(4)]
        a, b_, c, d = q[0] + q[2], q[0] - q[2], q[1] + q[3], q[1] - q[3]
        folded = (a + c, a - c, b_ + d, b_ - d)
        solved = []
        for i in range(4):
            y = dot3(split2(folded[i]), (forward[0, i], forward[1, i]))
            factor = scale[:, i * quad : (i + 1) * quad]
            y = (y.reshape(batch, box, quad) * factor[None]).reshape(batch * box, quad)
            solved.append(dot3(split2(y), (backward[0, i], backward[1, i])))
        ee, eo, oe, oo = solved
        a, b_, c, d = ee + oe, ee - oe, eo + oo, eo - oo
        field = jnp.concatenate([a + c, a - c, b_ + d, b_ - d], axis=1)
        v = dot3(split2(jnp.concatenate(lhs_back, 0)), split2(field))
        for i in range(batch):
            at = pl.ds(slots[which, 0, base + i] * frame, frame)
            lo = i * frame
            acc[at, :] = acc[at, :] + v[lo : lo + frame] * held[lo : lo + frame]
        return 0

    lax.fori_loop(0, (count[which] + batch - 1) // batch, step, 0)
    if first:
        return
    head, low = split2(acc[...])
    res = dot(head, ungroup[...]) + dot(low, ungroup[...])
    values, codes = coded(res)
    for m in range(z.own):
        for k in range(z.span):
            at = m * frame + k * z.rows
            outs[k][m] = values[at : at + z.rows].astype(i16)
            plane, lane = z.own + m * LANES // z.cells, m * LANES % z.cells
            outs[k][plane, :, lane : lane + LANES] = codes[at : at + z.rows].astype(i16)


def pair_part(z, ids, count, slots, mine, here, layout, pieces, sums=None):
    first = sums is None
    tables = pair_tables(z)
    smem = pl.BlockSpec(memory_space=pltpu.SMEM)
    vmem = pl.BlockSpec(memory_space=pltpu.VMEM)
    hbm = pl.BlockSpec(memory_space=pl.ANY)
    names = ("regroup", "forward", "backward", "scale", "into", "back") + (() if first else ("ungroup",))
    wide, total = z.batch * z.frame, (z.own * z.frame, z.cells)
    if first:
        given, shapes = [], jax.ShapeDtypeStruct(total, f32)
    else:
        given, shapes = [sums], [jax.ShapeDtypeStruct((z.planes, z.rows, z.cells), i16)] * z.span
    return pl.pallas_call(
        functools.partial(pair_kernel, z, first, layout),
        out_shape=shapes,
        in_specs=[smem] * 4 + [hbm] * (1 + len(pieces)) + [vmem] * (len(given) + len(names)),
        out_specs=vmem if first else [vmem] * z.span,
        scratch_shapes=[
            pltpu.VMEM((z.span, z.colors, z.rows, z.cells), bf16),
            pltpu.VMEM((wide, z.cells), f32),
            pltpu.VMEM((z.own, z.frame, z.cells), f32),
            pltpu.VMEM((wide, z.cells), f32),
            *([] if first else [pltpu.VMEM(total, f32)]),
            pltpu.SemaphoreType.DMA((1 + len(pieces),)),
        ],
        compiler_params=pltpu.CompilerParams(vmem_limit_bytes=34 << 20),
        cost_estimate=pl.CostEstimate(
            flops=8_000_000_000 if first else 20_000_000_000, bytes_accessed=16_000_000, transcendentals=0
        ),
        name="first_pairs" if first else "pair_solves",
    )(ids, count, slots, mine, here, *pieces, *given, *[jnp.asarray(tables[n]) for n in names])


def plane_kernel(z, per_step, here, potential, plane, out):
    centre = here[...].reshape(per_step * z.rows, z.cells)
    tile, reach = 256, stencil_reach * z.box
    cols = []
    for j in range(0, z.cells, tile):
        lo, hi = max(0, j - reach) // tile * tile, -(-min(z.cells, j + tile + reach) // tile) * tile
        u = centre[:, lo:hi]
        cols.append(dot(u, plane[0, lo:hi, j : j + tile]) + dot(u, plane[1, lo:hi, j : j + tile]))
    flat = jnp.concatenate(cols, axis=1).reshape(per_step, z.rows, z.cells)
    out[...] = flat + potential[...][None] * here[...].astype(f32)


def plane_part(z, here, potential, plane):
    per_step = kin_colors * max(d for d in (1, 2, 3, 4) if z.colors // kin_colors % d == 0)
    block = pl.BlockSpec((per_step, z.rows, z.cells), lambda i: (i, 0, 0))
    vmem = pl.BlockSpec(memory_space=pltpu.VMEM)
    return pl.pallas_call(
        functools.partial(plane_kernel, z, per_step),
        grid=(z.colors // per_step,),
        out_shape=jax.ShapeDtypeStruct((z.colors, z.rows, z.cells), f32),
        in_specs=[block, vmem, vmem],
        out_specs=block,
        compiler_params=pltpu.CompilerParams(
            vmem_limit_bytes=16 << 20, dimension_semantics=("arbitrary",)
        ),
        cost_estimate=pl.CostEstimate(flops=6_000_000_000, bytes_accessed=12_000_000, transcendentals=0),
        name="plane",
    )(here, potential, plane)


def along_kernel(z, per_step, layout, ids, shift, here, flat, *rest):
    pieces, rest = rest[: len(layout)], rest[len(layout) :]
    along, out, near, lhs, sems = rest
    q, g = ids[0], ids[1]
    step = pl.program_id(0)

    @pl.when(step == 0)
    def _():
        copies = []
        for piece, ref in zip(layout, pieces):
            to = near.at[(piece.slab(q) > z.mid).astype(i32), piece.colors(g)]
            copies.append(pltpu.make_async_copy(ref, to, sems.at[len(copies)]))
        for c in copies:
            c.start()
        for c in copies:
            c.wait()

    rows, cells, kc = z.rows, z.cells, kin_colors
    lane = lax.broadcasted_iota(i32, (rows, 3 * kc * rows), 1)
    for s in range(per_step // kc):
        first = step * per_step + s * kc
        for i in range(kc):
            start = lax.rem(shift[first + i] - q * rows + z.grid, z.box)
            lhs[i * rows : (i + 1) * rows, :] = jnp.where(lane // rows % kc == i, along[start], 0.0)
        mid = here[s * kc : (s + 1) * kc].reshape(kc * rows, cells)
        before = near[0, pl.ds(first, kc)].reshape(kc * rows, cells)
        after = near[1, pl.ds(first, kc)].reshape(kc * rows, cells)
        stack = jnp.concatenate([before, mid, after], axis=0)
        head, low = split2(lhs[...])
        kin = (dot(head, stack) + dot(low, stack)).reshape(kc, rows, cells)
        out[s * kc : (s + 1) * kc] = flat[s * kc : (s + 1) * kc] + kin


def along_part(z, ids, shift, here, flat, layout, pieces, along):
    per_step = kin_colors * max(d for d in (1, 2, 3, 4) if z.colors // kin_colors % d == 0)
    smem = pl.BlockSpec(memory_space=pltpu.SMEM)
    hbm = pl.BlockSpec(memory_space=pl.ANY)
    block = pl.BlockSpec((per_step, z.rows, z.cells), lambda i: (i, 0, 0))
    vmem = pl.BlockSpec(memory_space=pltpu.VMEM)
    return pl.pallas_call(
        functools.partial(along_kernel, z, per_step, layout),
        grid=(z.colors // per_step,),
        out_shape=jax.ShapeDtypeStruct((z.colors, z.rows, z.cells), f32),
        in_specs=[smem, smem, block, block] + [hbm] * len(pieces) + [vmem],
        out_specs=block,
        scratch_shapes=[
            pltpu.VMEM((2, z.colors, z.rows, z.cells), bf16),
            pltpu.VMEM((kin_colors * z.rows, 3 * kin_colors * z.rows), f32),
            pltpu.SemaphoreType.DMA((len(pieces),)),
        ],
        compiler_params=pltpu.CompilerParams(
            vmem_limit_bytes=16 << 20, dimension_semantics=("arbitrary",)
        ),
        cost_estimate=pl.CostEstimate(flops=5_000_000_000, bytes_accessed=12_000_000, transcendentals=0),
        name="along",
    )(ids, shift, here, flat, *pieces, along)


def finish_kernel(z, spans, ids, dst, local, *rest):
    parts, (out, total, sem) = rest[:-3], rest[-3:]
    order = butterfly_order(z.groups)
    at = 0
    for backs in spans:
        for p in range(z.groups):
            ref, at = parts[at], at + 1
            for b, back in enumerate(backs):
                for m in range(z.own):
                    c = dst[((ids[1] ^ order[p]) * z.width + back) * z.own + m]
                    plane, lane = z.own + m * LANES // z.cells, m * LANES % z.cells
                    scale = scale_of(ref[b * z.planes + plane, :, lane : lane + LANES])
                    value = ref[b * z.planes + m].astype(f32)
                    wide = jnp.concatenate([scale] * (z.cells // LANES), axis=1)
                    total[c] = local[c] + value * wide
                    pltpu.make_async_copy(total.at[c], out.at[c], sem).start()
    pltpu.make_async_copy(total, out, sem).wait()


def finish(z, ids, dst, local, spans, parts):
    smem = pl.BlockSpec(memory_space=pltpu.SMEM)
    vmem = pl.BlockSpec(memory_space=pltpu.VMEM)
    return pl.pallas_call(
        functools.partial(finish_kernel, z, spans),
        out_shape=jax.ShapeDtypeStruct(local.shape, f32),
        in_specs=[smem, smem, vmem] + [vmem] * len(parts),
        out_specs=pl.BlockSpec(memory_space=pl.ANY),
        scratch_shapes=[pltpu.VMEM(local.shape, f32), pltpu.SemaphoreType.DMA],
        compiler_params=pltpu.CompilerParams(vmem_limit_bytes=16 << 20),
        name="finish",
    )(ids, dst, local, *parts)


def moved(x, source, slabs):
    return lax.ppermute(x, "orb", [(source(i) % slabs, i) for i in range(slabs)])


def from_slab(x, away, slabs):
    return moved(x, lambda i: i + away, slabs)


def swapped(x, bit, groups):
    return lax.ppermute(x, "group", [(i, i ^ bit) for i in range(groups)])


def shared(piece, groups, *others):
    have, step = [piece], groups // 2
    while step:
        if step == 1 and others:
            have = [after(x, *others) for x in have]
        have += [swapped(x, step, groups) for x in have]
        step //= 2
    return have


def after(x, *others):
    return lax.optimization_barrier((x, *others))[0]


def fetch(z, orbitals, g, early_work, late_work, first_pairs):
    slabs, groups = z.slabs, z.groups
    layout, pieces = [], []

    if not z.staged:
        done = early_work()
        flat = late_work(orbitals)
        sums = first_pairs(done, [], [])
        quarter = lax.dynamic_slice_in_dim(orbitals, g * z.part, z.part, 0)
        for k in range(z.span):
            if k != z.mid:
                pieces += shared(from_slab(quarter, k - z.mid, slabs), groups)
                layout += [Piece(k, k, flip, groups, z.part, 0, z.part) for flip in butterfly_order(groups)]
        return layout, pieces, (*done, flat, sums)
    half, lo, hi = z.colors // 2, z.mid - 2, z.mid + 2
    mine = lax.dynamic_slice_in_dim(orbitals, lax.rem(g, 2) * half, half, 0)
    side = moved(mine, lambda i: i + 2 if i % 2 == 0 else i - 2, slabs)
    near = moved(mine, lambda i: i ^ 1, slabs)
    done = early_work()
    flat = late_work(after(orbitals, done[0]))
    side = after(side, *done, flat)
    far = moved(side, lambda i: i ^ 1, slabs)
    rest = moved(after(mine, flat), lambda i: i - 2 if i % 2 == 0 else i + 2, slabs)

    def keep(x, even, odd):
        for flip, y in enumerate((x, swapped(x, 1, groups))):
            layout.append(Piece(even, odd, flip, 2, half, 0, half))
            pieces.append(y)

    keep(near, lo + 3, lo + 1)
    keep(side, hi, lo)
    sums = first_pairs(done, list(layout), list(pieces))
    keep(after(far, sums), lo + 1, lo + 3)
    keep(after(rest, sums), lo, hi)
    return layout, pieces, (*done, flat, sums)


def body(orbitals, potential, box_shift, pair_partner, pair_member):
    slabs, groups = lax.axis_size("orb"), lax.axis_size("group")
    z = Sizes(orbitals, pair_partner, groups, slabs)
    q, g = lax.axis_index("orb"), lax.axis_index("group")
    ids = jnp.stack([q, g]).astype(i32)
    plane, along = [jnp.asarray(t) for t in stencil_tables(z)]
    layout, pieces, done = fetch(
        z,
        orbitals,
        g,
        lambda: plan(z, ids, box_shift, pair_partner, pair_member),
        lambda x: plane_part(z, x, potential, plane),
        lambda planned, layout, pieces: pair_part(z, ids, *planned[:3], orbitals, layout, pieces),
    )
    count, slots, home, dst, flat, sums = done
    spread = pair_part(z, ids, count, slots, home, orbitals, layout, pieces, sums)
    parts = [
        spread[k] if k == z.mid else from_slab(spread[k], z.mid - k, slabs) for k in range(z.span)
    ]
    parts[0] = parts[0] + parts[-1]
    spans = [(z.mid,), tuple(range(z.mid + 1, z.width)), tuple(range(z.mid))]
    middle = shared(parts[z.mid], groups)
    near = jnp.concatenate([parts[k] for k in spans[1]], axis=0)
    beside = [i for i, p in enumerate(layout) if {p.even, p.odd} <= {z.mid - 1, z.mid + 1}]
    local = along_part(
        z,
        ids,
        box_shift,
        orbitals,
        after(flat, near),
        [layout[i] for i in beside],
        [pieces[i] for i in beside],
        along,
    )
    far = jnp.concatenate([parts[k] for k in spans[2]], axis=0)
    near, far = shared(near, groups), shared(far, groups, local)
    return finish(z, ids, dst, local, spans, middle + near + far)


def solution(mesh):
    placed = (P(None, "orb", None), P("orb", None), P(), P(), P())
    return jax.shard_map(
        body, mesh=mesh, in_specs=placed, out_specs=P(None, "orb", None), check_vma=False
    )
```

```python
import functools
import math
from typing import NamedTuple

import jax
import jax.numpy as jnp
import numpy as np
from jax import lax
from jax.experimental import pallas as pl
from jax.experimental.pallas import tpu as pltpu
from jax.sharding import PartitionSpec as P

lap_weights = (
    -5369.0 / 1800.0,
    12.0 / 7.0,
    -15.0 / 56.0,
    10.0 / 189.0,
    -1.0 / 112.0,
    2.0 / 1925.0,
    -1.0 / 16632.0,
)
stencil_reach = 6
mixing = 0.25
f32, bf16, i32, i16 = jnp.float32, jnp.bfloat16, jnp.int32, jnp.int16
kin_colors = 8
EMPTY = -(1 << 20)
LANES = 128
TOP = 32767.0
STEPS = 256.0


def split_np(values):
    head = np.asarray(values, np.float32).astype(bf16)
    rest = (values - head.astype(np.float64)).astype(np.float32).astype(bf16)
    return np.stack([head, rest])


def split2(x):
    head = x.astype(bf16)
    return head, (x - head.astype(f32)).astype(bf16)


def dot(a, b):
    return jnp.dot(a, b, preferred_element_type=f32)


def dot3(a, b):
    rows = a[0].shape[0]
    both = dot(jnp.concatenate(a, axis=0), b[0])
    return both[:rows] + (dot(a[0], b[1]) + both[rows:])


class Sizes:
    def __init__(self, orbitals, pair_partner, groups, slabs):
        self.colors, self.rows, self.cells = orbitals.shape
        self.groups, self.slabs = groups, slabs
        self.box = math.isqrt(self.cells)
        self.width = self.box // self.rows
        self.span = self.width + 1
        self.mid = self.width // 2
        self.home = self.colors // self.width
        self.blocks = pair_partner.shape[0] // slabs
        self.members = self.home // self.blocks
        self.slots = pair_partner.shape[1]
        self.grid = slabs * self.rows
        self.per = self.grid // self.box
        self.part = self.colors // groups
        self.own = self.home // groups
        self.frame = self.span * self.rows
        self.batch = max(1, 256 // self.frame)
        self.planes = self.own + -(-self.own * LANES // self.cells)
        self.staged = self.mid == 2 and slabs % 2 == 0 and groups >= 2
        self.cap = -(-self.blocks * self.slots // self.batch) * self.batch + self.batch


def butterfly_order(groups):
    order, step = [0], groups // 2
    while step:
        order += [o ^ step for o in order]
        step //= 2
    return order


def sine_matrix(box):
    count = np.arange(1, box + 1)
    return np.sqrt(2.0 / (box + 1)) * np.sin(np.pi * np.outer(count, count) / (box + 1))


def pair_tables(z):
    box, half = z.box, z.box // 2
    sine = sine_matrix(box)
    side = [np.arange(half), box - 1 - np.arange(half)]
    order = np.concatenate([(y[:, None] * box + x[None, :]).reshape(-1) for y in side for x in side])
    regroup = np.zeros((z.cells, z.cells))
    regroup[order, np.arange(z.cells)] = 1.0
    halves = [sine[0::2, :half], sine[1::2, :half]]
    forward = np.stack([np.kron(a, b).T for a in halves for b in halves])
    backward = np.stack([m.T for m in forward])
    single = 2.0 - 2.0 * np.cos(np.pi * np.arange(1, box + 1) / (box + 1))
    modes = [(single[py::2][:, None] + single[pz::2][None, :]).reshape(-1) for py in (0, 1) for pz in (0, 1)]
    scale = -mixing / (single[:, None] + np.concatenate(modes)[None, :])
    into = np.zeros((z.rows, box, z.batch * z.frame))
    back = np.zeros((z.rows, z.frame, z.batch * box))
    for sub in range(z.rows):
        for i in range(z.batch):
            into[sub, :, i * z.frame + sub : i * z.frame + sub + box] = sine
            back[sub, sub : sub + box, i * box : (i + 1) * box] = sine.T
    return dict(
        regroup=regroup.astype(bf16),
        ungroup=regroup.T.astype(bf16),
        forward=split_np(forward),
        backward=split_np(backward),
        scale=scale.astype(np.float32),
        into=into.astype(np.float32),
        back=back.astype(np.float32),
    )


def stencil_tables(z):
    box, rows = z.box, z.rows
    band = np.zeros((box, box))
    for off in range(1, stencil_reach + 1):
        band += lap_weights[off] * (np.eye(box, k=off) + np.eye(box, k=-off))
    eye = np.eye(box)
    plane = -0.5 * (3.0 * lap_weights[0] * np.eye(z.cells) + np.kron(band, eye) + np.kron(eye, band))
    along = np.zeros((box, rows, 3 * kin_colors * rows))
    for start in range(box):
        for x in range(rows):
            for y in range(-rows, 2 * rows):
                off = abs(y - x)
                if off and off <= stencil_reach and (x - start) // box == (y - start) // box:
                    for i in range(kin_colors):
                        at = ((y + rows) // rows) * kin_colors * rows + i * rows + y % rows
                        along[start, x, at] = -0.5 * lap_weights[off]
    return split_np(plane), along.astype(np.float32)


def plan_kernel(z, ids, shift, partner, member, count_ref, slot_ref, mine_ref, dst_ref, order, filled):
    q, g = ids[0], ids[1]
    o = lax.rem(q + z.slabs - z.mid, z.slabs)
    for c in range(z.width):
        filled[c] = 0

    def color_step(c, _):
        cls = shift[c] // z.rows
        n = filled[cls]
        filled[cls] = n + 1
        order[cls, n] = c
        back = lax.rem(q - cls + z.slabs * z.width, z.width)
        dst_ref[(lax.rem(n, z.groups) * z.width + back) * z.own + n // z.groups] = c
        return 0

    lax.fori_loop(0, z.colors, color_step, 0)
    home_class = lax.rem(o, z.width)
    for m in range(z.own):
        c = order[home_class, m * z.groups + g]
        mine_ref[0, m] = c
        mine_ref[1, m] = lax.rem(shift[c], z.rows)
    reach_slots = z.slots // (2 * z.width - 1)
    sign = jnp.where(lax.rem(q, 2) == 0, 1, -1)
    counts = (jnp.int32(0), jnp.int32(0))
    for t in range(z.blocks):

        def slot_step(p, counts, t=t):
            j = partner[o * z.blocks + t, p]
            n = t * z.members + member[o * z.blocks + t, p]
            live = jnp.logical_and(j >= 0, lax.rem(n, z.groups) == g)
            j = jnp.maximum(j, 0)
            cj = j // z.per
            sub = lax.rem(shift[order[home_class, n]], z.rows)
            there = (j - cj * z.per) * z.box + shift[cj]
            d = there - (o * z.rows + sub) + z.grid // 2
            d = lax.rem(d + z.grid, z.grid) - z.grid // 2
            reach = (p // reach_slots - (z.width - 1)) * sign
            first = jnp.logical_and(reach >= z.mid, z.staged).astype(i32)
            at = jnp.where(first == 1, counts[0], counts[1])
            slot_ref[first, 0, at] = n // z.groups
            slot_ref[first, 1, at] = cj
            slot_ref[first, 2, at] = sub + d
            slot_ref[first, 3, at] = sub
            one = live.astype(i32)
            return counts[0] + one * first, counts[1] + one * (1 - first)

        counts = lax.fori_loop(0, z.slots, slot_step, counts)
    for first in (0, 1):
        total = counts[1 - first]
        count_ref[first] = total
        for i in range(z.batch):
            slot_ref[first, 0, total + i] = 0
            slot_ref[first, 1, total + i] = 0
            slot_ref[first, 2, total + i] = EMPTY
            slot_ref[first, 3, total + i] = 0


def plan(z, ids, shift, partner, member):
    smem = pl.BlockSpec(memory_space=pltpu.SMEM)
    return pl.pallas_call(
        functools.partial(plan_kernel, z),
        out_shape=(
            jax.ShapeDtypeStruct((2,), i32),
            jax.ShapeDtypeStruct((2, 4, z.cap), i32),
            jax.ShapeDtypeStruct((2, z.own), i32),
            jax.ShapeDtypeStruct((z.colors,), i32),
        ),
        in_specs=[smem] * 4,
        out_specs=(smem,) * 4,
        scratch_shapes=[pltpu.SMEM((z.width, z.colors), i32), pltpu.SMEM((z.width,), i32)],
        cost_estimate=pl.CostEstimate(flops=10_000_000_000, bytes_accessed=100_000, transcendentals=0),
        name="plan",
    )(ids, shift, partner, member)


class Piece(NamedTuple):
    even: int
    odd: int
    flip: int
    parts: int
    unit: int
    add: int
    size: int

    def slab(self, q):
        return jnp.where(lax.rem(q, 2) == 0, self.even, self.odd)

    def colors(self, g):
        return pl.ds(lax.rem(g ^ self.flip, self.parts) * self.unit + self.add, self.size)


def scale_of(code):
    return jnp.exp2(code.astype(f32) * (1.0 / STEPS)) * (1.0 / TOP)


def coded(x):
    groups = [x[:, i : i + LANES] for i in range(0, x.shape[1], LANES)]
    top = functools.reduce(jnp.maximum, [jnp.abs(v) for v in groups])
    code = jnp.ceil(jnp.log2(jnp.clip(top, 2.0**-100, 2.0**100)) * STEPS) + 1.0
    factor = 1.0 / scale_of(code)
    whole = [jnp.clip(jnp.round(v * factor), -TOP, TOP).astype(i32) for v in groups]
    return jnp.concatenate(whole, axis=1), jnp.where(top > 0, code, 0.0).astype(i32)


def pair_kernel(z, first, layout, ids, count, slots, mine, here, *rest):
    pieces, rest = rest[: len(layout)], rest[len(layout) :]
    if not first:
        sums, rest = rest[0], rest[1:]
    (regroup, forward, backward, scale, into, back), rest = rest[:6], rest[6:]
    if first:
        acc, window, raw, own, held, sems = rest
    else:
        ungroup, outs, (window, raw, own, held, acc, sems) = rest[0], rest[1 : z.span + 1], rest[z.span + 1 :]
    which = 1 if first else 0
    q, g = ids[0], ids[1]
    copies = [pltpu.make_async_copy(here, window.at[z.mid], sems.at[0])]
    for piece, ref in zip(layout, pieces):
        to = window.at[piece.slab(q), piece.colors(g)]
        copies.append(pltpu.make_async_copy(ref, to, sems.at[len(copies)]))
    for c in copies:
        c.start()
    acc[...] = jnp.zeros(acc.shape, f32) if first else sums[...]
    for c in copies:
        c.wait()
    frame, box, batch, quad = z.frame, z.box, z.batch, z.cells // 4
    rows = lax.broadcasted_iota(i32, (z.rows, z.cells), 0)

    def regrouped():
        return dot(raw[...].astype(bf16), regroup[...])

    for start in range(0, z.own, batch):
        todo = min(batch, z.own - start)
        for i in range(batch):
            for k in range(z.span):
                at = i * frame + k * z.rows
                if i < todo:
                    value = window[k, mine[0, start + i]].astype(f32)
                    if first and k != z.mid:
                        here_now = (k > z.mid) == (lax.rem(q, 2) == 0)
                        value = jnp.where(here_now, value, 0.0)
                    raw[at : at + z.rows, :] = value
                else:
                    raw[at : at + z.rows, :] = jnp.zeros((z.rows, z.cells), f32)
        done = regrouped()
        for i in range(todo):
            own[start + i] = done[i * frame : (i + 1) * frame]

    lane_in = lax.broadcasted_iota(i32, (box, batch * frame), 1)
    lane_back = lax.broadcasted_iota(i32, (frame, batch * box), 1)

    def step(b, _):
        base = b * batch
        for i in range(batch):
            color, start = slots[which, 1, base + i], slots[which, 2, base + i]
            for k in range(z.span):
                at = i * frame + k * z.rows
                r = rows + (k * z.rows - start)
                inside = (r >= 0) & (r < box)
                raw[at : at + z.rows, :] = jnp.where(inside, window[k, color].astype(f32), 0.0)
        held[...] = regrouped()
        lhs_in, lhs_back, density = [], [], []
        for i in range(batch):
            m, sub = slots[which, 0, base + i], slots[which, 3, base + i]
            lo = i * frame
            lhs_in.append(jnp.where((lane_in >= lo) & (lane_in < lo + frame), into[sub], 0.0))
            lo = i * box
            lhs_back.append(jnp.where((lane_back >= lo) & (lane_back < lo + box), back[sub], 0.0))
            density.append(own[m] * held[i * frame : (i + 1) * frame])
        x = dot3(split2(jnp.concatenate(lhs_in, 0)), split2(jnp.concatenate(density, 0)))
        q = [x[:, i * quad : (i + 1) * quad] for i in range(4)]
        a, b_, c, d = q[0] + q[2], q[0] - q[2], q[1] + q[3], q[1] - q[3]
        folded = (a + c, a - c, b_ + d, b_ - d)
        solved = []
        for i in range(4):
            y = dot3(split2(folded[i]), (forward[0, i], forward[1, i]))
            factor = scale[:, i * quad : (i + 1) * quad]
            y = (y.reshape(batch, box, quad) * factor[None]).reshape(batch * box, quad)
            solved.append(dot3(split2(y), (backward[0, i], backward[1, i])))
        ee, eo, oe, oo = solved
        a, b_, c, d = ee + oe, ee - oe, eo + oo, eo - oo
        field = jnp.concatenate([a + c, a - c, b_ + d, b_ - d], axis=1)
        v = dot3(split2(jnp.concatenate(lhs_back, 0)), split2(field))
        for i in range(batch):
            at = pl.ds(slots[which, 0, base + i] * frame, frame)
            lo = i * frame
            acc[at, :] = acc[at, :] + v[lo : lo + frame] * held[lo : lo + frame]
        return 0

    lax.fori_loop(0, (count[which] + batch - 1) // batch, step, 0)
    if first:
        return
    head, low = split2(acc[...])
    res = dot(head, ungroup[...]) + dot(low, ungroup[...])
    values, codes = coded(res)
    for m in range(z.own):
        for k in range(z.span):
            at = m * frame + k * z.rows
            outs[k][m] = values[at : at + z.rows].astype(i16)
            plane, lane = z.own + m * LANES // z.cells, m * LANES % z.cells
            outs[k][plane, :, lane : lane + LANES] = codes[at : at + z.rows].astype(i16)


def pair_part(z, ids, count, slots, mine, here, layout, pieces, sums=None):
    first = sums is None
    tables = pair_tables(z)
    smem = pl.BlockSpec(memory_space=pltpu.SMEM)
    vmem = pl.BlockSpec(memory_space=pltpu.VMEM)
    hbm = pl.BlockSpec(memory_space=pl.ANY)
    names = ("regroup", "forward", "backward", "scale", "into", "back") + (() if first else ("ungroup",))
    wide, total = z.batch * z.frame, (z.own * z.frame, z.cells)
    if first:
        given, shapes = [], jax.ShapeDtypeStruct(total, f32)
    else:
        given, shapes = [sums], [jax.ShapeDtypeStruct((z.planes, z.rows, z.cells), i16)] * z.span
    return pl.pallas_call(
        functools.partial(pair_kernel, z, first, layout),
        out_shape=shapes,
        in_specs=[smem] * 4 + [hbm] * (1 + len(pieces)) + [vmem] * (len(given) + len(names)),
        out_specs=vmem if first else [vmem] * z.span,
        scratch_shapes=[
            pltpu.VMEM((z.span, z.colors, z.rows, z.cells), bf16),
            pltpu.VMEM((wide, z.cells), f32),
            pltpu.VMEM((z.own, z.frame, z.cells), f32),
            pltpu.VMEM((wide, z.cells), f32),
            *([] if first else [pltpu.VMEM(total, f32)]),
            pltpu.SemaphoreType.DMA((1 + len(pieces),)),
        ],
        compiler_params=pltpu.CompilerParams(vmem_limit_bytes=34 << 20),
        cost_estimate=pl.CostEstimate(
            flops=8_000_000_000 if first else 20_000_000_000, bytes_accessed=16_000_000, transcendentals=0
        ),
        name="first_pairs" if first else "pair_solves",
    )(ids, count, slots, mine, here, *pieces, *given, *[jnp.asarray(tables[n]) for n in names])


def plane_kernel(z, per_step, here, potential, plane, out):
    centre = here[...].reshape(per_step * z.rows, z.cells)
    tile, reach = 256, stencil_reach * z.box
    cols = []
    for j in range(0, z.cells, tile):
        lo, hi = max(0, j - reach) // tile * tile, -(-min(z.cells, j + tile + reach) // tile) * tile
        u = centre[:, lo:hi]
        cols.append(dot(u, plane[0, lo:hi, j : j + tile]) + dot(u, plane[1, lo:hi, j : j + tile]))
    flat = jnp.concatenate(cols, axis=1).reshape(per_step, z.rows, z.cells)
    out[...] = flat + potential[...][None] * here[...].astype(f32)


def plane_part(z, here, potential, plane):
    per_step = kin_colors * max(d for d in (1, 2, 3, 4) if z.colors // kin_colors % d == 0)
    block = pl.BlockSpec((per_step, z.rows, z.cells), lambda i: (i, 0, 0))
    vmem = pl.BlockSpec(memory_space=pltpu.VMEM)
    return pl.pallas_call(
        functools.partial(plane_kernel, z, per_step),
        grid=(z.colors // per_step,),
        out_shape=jax.ShapeDtypeStruct((z.colors, z.rows, z.cells), f32),
        in_specs=[block, vmem, vmem],
        out_specs=block,
        compiler_params=pltpu.CompilerParams(
            vmem_limit_bytes=16 << 20, dimension_semantics=("arbitrary",)
        ),
        cost_estimate=pl.CostEstimate(flops=6_000_000_000, bytes_accessed=12_000_000, transcendentals=0),
        name="plane",
    )(here, potential, plane)


def along_kernel(z, per_step, layout, ids, shift, here, flat, *rest):
    pieces, rest = rest[: len(layout)], rest[len(layout) :]
    along, out, near, lhs, sems = rest
    q, g = ids[0], ids[1]
    step = pl.program_id(0)

    @pl.when(step == 0)
    def _():
        copies = []
        for piece, ref in zip(layout, pieces):
            to = near.at[(piece.slab(q) > z.mid).astype(i32), piece.colors(g)]
            copies.append(pltpu.make_async_copy(ref, to, sems.at[len(copies)]))
        for c in copies:
            c.start()
        for c in copies:
            c.wait()

    rows, cells, kc = z.rows, z.cells, kin_colors
    lane = lax.broadcasted_iota(i32, (rows, 3 * kc * rows), 1)
    for s in range(per_step // kc):
        first = step * per_step + s * kc
        for i in range(kc):
            start = lax.rem(shift[first + i] - q * rows + z.grid, z.box)
            lhs[i * rows : (i + 1) * rows, :] = jnp.where(lane // rows % kc == i, along[start], 0.0)
        mid = here[s * kc : (s + 1) * kc].reshape(kc * rows, cells)
        before = near[0, pl.ds(first, kc)].reshape(kc * rows, cells)
        after = near[1, pl.ds(first, kc)].reshape(kc * rows, cells)
        stack = jnp.concatenate([before, mid, after], axis=0)
        head, low = split2(lhs[...])
        kin = (dot(head, stack) + dot(low, stack)).reshape(kc, rows, cells)
        out[s * kc : (s + 1) * kc] = flat[s * kc : (s + 1) * kc] + kin


def along_part(z, ids, shift, here, flat, layout, pieces, along):
    per_step = kin_colors * max(d for d in (1, 2, 3, 4) if z.colors // kin_colors % d == 0)
    smem = pl.BlockSpec(memory_space=pltpu.SMEM)
    hbm = pl.BlockSpec(memory_space=pl.ANY)
    block = pl.BlockSpec((per_step, z.rows, z.cells), lambda i: (i, 0, 0))
    vmem = pl.BlockSpec(memory_space=pltpu.VMEM)
    return pl.pallas_call(
        functools.partial(along_kernel, z, per_step, layout),
        grid=(z.colors // per_step,),
        out_shape=jax.ShapeDtypeStruct((z.colors, z.rows, z.cells), f32),
        in_specs=[smem, smem, block, block] + [hbm] * len(pieces) + [vmem],
        out_specs=block,
        scratch_shapes=[
            pltpu.VMEM((2, z.colors, z.rows, z.cells), bf16),
            pltpu.VMEM((kin_colors * z.rows, 3 * kin_colors * z.rows), f32),
            pltpu.SemaphoreType.DMA((len(pieces),)),
        ],
        compiler_params=pltpu.CompilerParams(
            vmem_limit_bytes=16 << 20, dimension_semantics=("arbitrary",)
        ),
        cost_estimate=pl.CostEstimate(flops=5_000_000_000, bytes_accessed=12_000_000, transcendentals=0),
        name="along",
    )(ids, shift, here, flat, *pieces, along)


def finish_kernel(z, spans, ids, dst, local, *rest):
    parts, (out, total, sem) = rest[:-3], rest[-3:]
    order = butterfly_order(z.groups)
    at = 0
    for backs in spans:
        for p in range(z.groups):
            ref, at = parts[at], at + 1
            for b, back in enumerate(backs):
                for m in range(z.own):
                    c = dst[((ids[1] ^ order[p]) * z.width + back) * z.own + m]
                    plane, lane = z.own + m * LANES // z.cells, m * LANES % z.cells
                    scale = scale_of(ref[b * z.planes + plane, :, lane : lane + LANES])
                    value = ref[b * z.planes + m].astype(f32)
                    wide = jnp.concatenate([scale] * (z.cells // LANES), axis=1)
                    total[c] = local[c] + value * wide
                    pltpu.make_async_copy(total.at[c], out.at[c], sem).start()
    pltpu.make_async_copy(total, out, sem).wait()


def finish(z, ids, dst, local, spans, parts):
    smem = pl.BlockSpec(memory_space=pltpu.SMEM)
    vmem = pl.BlockSpec(memory_space=pltpu.VMEM)
    return pl.pallas_call(
        functools.partial(finish_kernel, z, spans),
        out_shape=jax.ShapeDtypeStruct(local.shape, f32),
        in_specs=[smem, smem, vmem] + [vmem] * len(parts),
        out_specs=pl.BlockSpec(memory_space=pl.ANY),
        scratch_shapes=[pltpu.VMEM(local.shape, f32), pltpu.SemaphoreType.DMA],
        compiler_params=pltpu.CompilerParams(vmem_limit_bytes=16 << 20),
        name="finish",
    )(ids, dst, local, *parts)


def moved(x, source, slabs):
    return lax.ppermute(x, "orb", [(source(i) % slabs, i) for i in range(slabs)])


def from_slab(x, away, slabs):
    return moved(x, lambda i: i + away, slabs)


def swapped(x, bit, groups):
    return lax.ppermute(x, "group", [(i, i ^ bit) for i in range(groups)])


def shared(piece, groups, *others):
    have, step = [piece], groups // 2
    while step:
        if step == 1 and others:
            have = [after(x, *others) for x in have]
        have += [swapped(x, step, groups) for x in have]
        step //= 2
    return have


def after(x, *others):
    return lax.optimization_barrier((x, *others))[0]


def fetch(z, orbitals, g, early_work, late_work, first_pairs):
    slabs, groups = z.slabs, z.groups
    layout, pieces = [], []

    if not z.staged:
        done = early_work()
        flat = late_work(orbitals)
        sums = first_pairs(done, [], [])
        quarter = lax.dynamic_slice_in_dim(orbitals, g * z.part, z.part, 0)
        for k in range(z.span):
            if k != z.mid:
                pieces += shared(from_slab(quarter, k - z.mid, slabs), groups)
                layout += [Piece(k, k, flip, groups, z.part, 0, z.part) for flip in butterfly_order(groups)]
        return layout, pieces, (*done, flat, sums)
    half, lo, hi = z.colors // 2, z.mid - 2, z.mid + 2
    mine = lax.dynamic_slice_in_dim(orbitals, lax.rem(g, 2) * half, half, 0)
    side = moved(mine, lambda i: i + 2 if i % 2 == 0 else i - 2, slabs)
    near = moved(mine, lambda i: i ^ 1, slabs)
    done = early_work()
    flat = late_work(after(orbitals, done[0]))
    side = after(side, *done, flat)
    far = moved(side, lambda i: i ^ 1, slabs)
    rest = moved(after(mine, flat), lambda i: i - 2 if i % 2 == 0 else i + 2, slabs)

    def keep(x, even, odd):
        for flip, y in enumerate((x, swapped(x, 1, groups))):
            layout.append(Piece(even, odd, flip, 2, half, 0, half))
            pieces.append(y)

    keep(near, lo + 3, lo + 1)
    keep(side, hi, lo)
    sums = first_pairs(done, list(layout), list(pieces))
    keep(after(far, sums), lo + 1, lo + 3)
    keep(after(rest, sums), lo, hi)
    return layout, pieces, (*done, flat, sums)


def body(orbitals, potential, box_shift, pair_partner, pair_member):
    slabs, groups = lax.axis_size("orb"), lax.axis_size("group")
    z = Sizes(orbitals, pair_partner, groups, slabs)
    q, g = lax.axis_index("orb"), lax.axis_index("group")
    ids = jnp.stack([q, g]).astype(i32)
    plane, along = [jnp.asarray(t) for t in stencil_tables(z)]
    layout, pieces, done = fetch(
        z,
        orbitals,
        g,
        lambda: plan(z, ids, box_shift, pair_partner, pair_member),
        lambda x: plane_part(z, x, potential, plane),
        lambda planned, layout, pieces: pair_part(z, ids, *planned[:3], orbitals, layout, pieces),
    )
    count, slots, home, dst, flat, sums = done
    spread = pair_part(z, ids, count, slots, home, orbitals, layout, pieces, sums)
    parts = [
        spread[k] if k == z.mid else from_slab(spread[k], z.mid - k, slabs) for k in range(z.span)
    ]
    parts[0] = parts[0] + parts[-1]
    spans = [(z.mid,), tuple(range(z.mid + 1, z.width)), tuple(range(z.mid))]
    middle = shared(parts[z.mid], groups)
    near = jnp.concatenate([parts[k] for k in spans[1]], axis=0)
    nears = shared(near, groups)
    beside = [i for i, p in enumerate(layout) if {p.even, p.odd} <= {z.mid - 1, z.mid + 1}]
    local = along_part(
        z,
        ids,
        box_shift,
        orbitals,
        after(flat, nears[min(1, groups - 1)]),
        [layout[i] for i in beside],
        [pieces[i] for i in beside],
        along,
    )
    far = jnp.concatenate([parts[k] for k in spans[2]], axis=0)
    near, far = nears, shared(far, groups, local)
    return finish(z, ids, dst, local, spans, middle + near + far)


def solution(mesh):
    placed = (P(None, "orb", None), P("orb", None), P(), P(), P())
    return jax.shard_map(
        body, mesh=mesh, in_specs=placed, out_specs=P(None, "orb", None), check_vma=False
    )
```
